256 devices in a mesh: row: 16 (over y, x_hi, core), col: 16 (over x_lo, z).
Axes of the slice: x: 4 (x_hi: 2, x_lo: 2; x = x_hi * 2 + x_lo), y: 4, z: 8, core: 2. Of those that a mesh axis runs over, the one named last changes fastest.
Arguments:
- tokens: bfloat16 [1280, 10240], P('col', 'row'), may hold values from -6 to 6
- up_weight: bfloat16 [10240, 20480], P('row', 'col'), may hold values from -0.0625 to 0.0625
- down_weight: bfloat16 [20480, 10240], P('col', 'row'), may hold values from -0.0390625 to 0.0390625
- grad_out: bfloat16 [1280, 10240], P('col', 'row'), may hold values from -6 to 6
Outputs:
- mixed: bfloat16 [1280, 10240], P('col', 'row')
- input_grad: bfloat16 [1280, 10240], P('col', 'row')
- up_grad: bfloat16 [10240, 20480], P('row', 'col')
- down_grad: bfloat16 [20480, 10240], P('col', 'row')
The draws below stay inside these ranges and needn't reach their ends.
All inputs are finite; a program needn't handle non-finite values.
Results may differ from the reference program's by a relative error of at most 0.005.
Values may be sent and summed in bfloat16 or wider, within the bound.
A program may use at most 128 MiB of HBM per device.

```python
import jax
import jax.numpy as jnp

D = 10240
FF = 20480
TOKENS = 1280


def levels(key, shape, pieces, smallest, largest):
    factor_of = 1.0
    for dim, shards_of in pieces:
        steps = jax.random.uniform(jax.random.fold_in(jax.random.fold_in(key, 6), dim), (shards_of,), jnp.float32, smallest / len(pieces), largest / len(pieces))
        factor_of = factor_of * jnp.repeat(jnp.exp(steps), shape[dim] // shards_of).reshape((-1,) + (1,) * (len(shape) - 1 - dim))
    return factor_of


def normal_values(rng, dims, deviation, most, pieces=(), held_as=jnp.bfloat16):
    factor_of = levels(rng, dims, pieces, -0.22, 0.18) if pieces else 1.0
    array = jax.random.normal(rng, dims, jnp.float32) * deviation * factor_of
    return jnp.minimum(jnp.maximum(array, -most), most).astype(held_as)


def setup_inputs(seed: int = 0) -> dict:
    streams_of = jax.random.split(jax.random.key(seed), 5)
    return {
        "tokens": normal_values(streams_of[0], (TOKENS, D), 1.0, 6.0, ((0, 16), (1, 16))),
        "up_weight": normal_values(streams_of[1], (D, FF), D ** -0.5, 0.0625, ((0, 16), (1, 16))),
        "down_weight": normal_values(streams_of[2], (FF, D), FF ** -0.5, 0.0390625, ((0, 16), (1, 16))),
        "grad_out": normal_values(streams_of[3], (TOKENS, D), 1.0, 6.0, ((0, 16), (1, 16))),
    }


def reference(tokens, up_weight, down_weight, grad_out):
    hidden = jnp.dot(tokens, up_weight, preferred_element_type=jnp.float32)
    active = jax.nn.gelu(hidden).astype(jnp.bfloat16)
    mixed = jnp.dot(active, down_weight, preferred_element_type=jnp.float32).astype(jnp.bfloat16)
    act_grad = jnp.dot(grad_out, down_weight.T, preferred_element_type=jnp.float32)
    _, pullback = jax.vjp(jax.nn.gelu, hidden)
    hidden_grad = pullback(act_grad)[0].astype(jnp.bfloat16)
    down_grad = jnp.dot(active.T, grad_out, preferred_element_type=jnp.float32).astype(jnp.bfloat16)
    input_grad = jnp.dot(hidden_grad, up_weight.T, preferred_element_type=jnp.float32).astype(jnp.bfloat16)
    up_grad = jnp.dot(tokens.T, hidden_grad, preferred_element_type=jnp.float32).astype(jnp.bfloat16)
    return (mixed, input_grad, up_grad, down_grad)
```

```python
import jax
import jax.numpy as jnp
from jax import lax
from jax.experimental import pallas as pl
from jax.experimental.pallas import tpu as pltpu
from jax.sharding import PartitionSpec as P

MESH = pl.DeviceIdType.MESH
BF = jnp.bfloat16
F32 = jnp.float32

TOK = 80
HALF = 640
WIDE = 1280
ROWS = 8 * TOK

PLACE = {0: 0, 1: 1, -1: 2, 2: 3, -2: 4, 3: 5, -3: 6, 4: 7}

C0 = 0.7978845608028654
C1 = 0.044715


def gelu(v):
    return 0.5 * v * (1.0 + jnp.tanh(C0 * (v + C1 * v * v * v)))


def gelu_slope(v):
    t = jnp.tanh(C0 * (v + C1 * v * v * v))
    return 0.5 * (1.0 + t) + 0.5 * v * (1.0 - t * t) * (C0 * (1.0 + 3.0 * C1 * v * v))


def rows_of(place):
    if isinstance(place, int):
        return pl.ds(place * TOK, TOK)
    return pl.ds(pl.multiple_of(place * TOK, TOK), TOK)


def cols_of(half):
    if isinstance(half, int):
        return pl.ds(half * HALF, HALF)
    return pl.ds(pl.multiple_of(half * HALF, HALF), HALF)


def kernel(
    tok_in, up_in, down_in, grad_in,
    mixed_out, igrad_out, upg_out, downg_out,
    up, down, tok, grad, act, hgrad, tok_o, grad_o,
    part, hid, p_send, p_recv, p_out, p_in, z_send, z_recv, f_send, f_recv,
    upg, downg, small,
    ssem, rsem, lsem,
):
    r, c = lax.axis_index("row"), lax.axis_index("col")
    y, xh, k = r // 4, (r // 2) % 2, r % 2
    xl, z = c // 8, c % 8

    def row_id(yy, hh, kk):
        return (yy * 2 + hh) * 2 + kk

    mate = (row_id(y, xh, 1 - k), c)
    yp = (row_id((y + 1) % 4, xh, k), c)
    ym = (row_id((y + 3) % 4, xh, k), c)
    across = (row_id(y, 1 - xh, k), c)
    zp = (r, xl * 8 + (z + 1) % 8)
    zm = (r, xl * 8 + (z + 7) % 8)
    other_c = (1 - xl) * 8 + z
    other0 = (row_id(y, xh, 0), other_c)
    other1 = (row_id(y, xh, 1), other_c)

    sends = []
    count = [0]

    def sem():
        count[0] += 1
        return count[0] - 1

    def rcopy(src, dst, dev):
        i = sem()
        cp = pltpu.make_async_remote_copy(
            src_ref=src, dst_ref=dst, send_sem=ssem.at[i], recv_sem=rsem.at[i],
            device_id=dev, device_id_type=MESH,
        )
        cp.start()
        sends.append(cp)
        return cp

    lcount = [0]

    def lcopy(src, dst):
        cp = pltpu.make_async_copy(src, dst, lsem.at[lcount[0]])
        lcount[0] += 1
        cp.start()
        return cp

    own_up = lcopy(up_in, up.at[pl.ds(pl.multiple_of(k * HALF, HALF), HALF)])
    own_down = lcopy(down_in, down.at[:, cols_of(k)])

    barrier = pltpu.get_barrier_semaphore()
    for dev in (mate, yp, ym, across, zp, zm, other0, other1):
        pl.semaphore_signal(barrier, inc=1, device_id=dev, device_id_type=MESH)
    pl.semaphore_wait(barrier, 8)

    def spread(src, buf):
        i, j = sem(), sem()
        dst = buf.at[rows_of(0), cols_of(k)]
        far = pltpu.make_async_remote_copy(
            src_ref=src, dst_ref=dst, send_sem=ssem.at[i], recv_sem=rsem.at[i + k],
            device_id=(row_id(y, xh, xl), other_c), device_id_type=MESH,
        )
        near = pltpu.make_async_remote_copy(
            src_ref=src, dst_ref=dst, send_sem=ssem.at[j], recv_sem=rsem.at[i + k],
            device_id=mate, device_id_type=MESH,
        )
        stay = pltpu.make_async_copy(src, dst, rsem.at[i + k])
        far.start()

        @pl.when(k != xl)
        def _():
            near.start()

        @pl.when(k == xl)
        def _():
            stay.start()

        def arrived(h):
            pltpu.make_async_copy(src, buf.at[rows_of(0), cols_of(h)], rsem.at[i + h]).wait()

        def sent():
            far.wait_send()

            @pl.when(k != xl)
            def _():
                near.wait_send()

        return arrived, sent

    tok_arrived, tok_sent = spread(tok_in, tok)
    w1 = rcopy(up_in, up.at[pl.ds(pl.multiple_of(k * HALF, HALF), HALF)], mate)
    w2 = rcopy(down_in, down.at[:, cols_of(k)], mate)
    grad_arrived, grad_sent = spread(grad_in, grad)

    class Gather:
        def __init__(self, buf, arrived):
            self.buf, self.arrived, self.got = buf, arrived, {}

        def piece(self, off, h):
            return self.buf.at[rows_of(PLACE[off]), cols_of(h)]

        def send(self, off, h, sign):
            to = off - sign
            if to == -4:
                to = 4
            cp = rcopy(self.piece(off, h), self.piece(to, h), zp if sign > 0 else zm)
            self.got[(to, h)] = cp

        def wait(self, off, h):
            cp = self.got.pop((off, h), None)
            if cp is not None:
                cp.wait_recv()

        def step(self, n):
            if n == 1:
                for h in (0, 1):
                    self.arrived(h)
                    self.send(0, h, 1)
                    self.send(0, h, -1)
            elif n < 4:
                for h in (0, 1):
                    self.wait(-(n - 1), h)
                    self.send(-(n - 1), h, 1)
                    self.wait(n - 1, h)
                    self.send(n - 1, h, -1)
            else:
                self.wait(-3, 0)
                self.send(-3, 0, 1)
                self.wait(3, 1)
                self.send(3, 1, -1)
                self.wait(-3, 1)
                self.wait(3, 0)

        def finish(self):
            self.wait(4, 0)
            self.wait(4, 1)

    def matmul(lhs, rhs, out, place, trans):
        rows = rows_of(place)

        def body(n, _):
            cols = pl.ds(pl.multiple_of(n * 256, 256), 256)
            if trans:
                v = lax.dot_general(lhs[rows, :], rhs[cols, :], (((1,), (1,)), ((), ())),
                                    preferred_element_type=F32)
            else:
                v = jnp.dot(lhs[rows, :], rhs[:, cols], preferred_element_type=F32)
            out[rows, cols] = v
            return 0

        lax.fori_loop(0, WIDE // 256, body, 0)

    class Reduce:
        def __init__(self, src, n):
            self.src, self.n, self.cp = src, n, {}

        def at(self, b, i):
            return rows_of((self.n * 2 + b) * 3 + i)

        def step1(self, b):
            s = rows_of(b * 4 + (y + 2) % 4)
            p_send[self.at(b, 0), :] = self.src[s, :].astype(BF)
            self.cp[(b, 1)] = [
                rcopy(p_send.at[self.at(b, 0), cols_of(0)], p_recv.at[self.at(b, 0), cols_of(0)], yp),
                rcopy(p_send.at[self.at(b, 0), cols_of(1)], p_recv.at[self.at(b, 0), cols_of(1)], ym),
            ]

        def step2(self, b):
            lo, hi = cols_of(0), cols_of(1)
            plus, minus = rows_of(b * 4 + (y + 1) % 4), rows_of(b * 4 + (y + 3) % 4)
            p_send[self.at(b, 1), hi] = self.src[plus, hi].astype(BF)
            p_send[self.at(b, 2), lo] = self.src[minus, lo].astype(BF)
            self.cp[(b, 1)][0].wait_recv()
            p_send[self.at(b, 1), lo] = (
                self.src[plus, lo] + p_recv[self.at(b, 0), lo].astype(F32)).astype(BF)
            first = rcopy(p_send.at[self.at(b, 1)], p_recv.at[self.at(b, 1)], yp)
            self.cp[(b, 1)][1].wait_recv()
            p_send[self.at(b, 2), hi] = (
                self.src[minus, hi] + p_recv[self.at(b, 0), hi].astype(F32)).astype(BF)
            second = rcopy(p_send.at[self.at(b, 2)], p_recv.at[self.at(b, 2)], ym)
            self.cp[(b, 2)] = [first, second]

        def total(self, b):
            for cp in self.cp[(b, 2)]:
                cp.wait_recv()
            return (self.src[rows_of(b * 4 + y), :] + p_recv[self.at(b, 1), :].astype(F32)
                    + p_recv[self.at(b, 2), :].astype(F32))

        def cross(self, b):
            t = self.total(b)

            @pl.when(xh == b)
            def _():
                hid[rows_of(self.n), :] = t

            @pl.when(xh != b)
            def _():
                p_out[rows_of(self.n), :] = t

        def send(self):
            self.x = rcopy(p_out.at[rows_of(self.n)], p_in.at[rows_of(self.n)], across)

        def result(self):
            self.x.wait_recv()
            return hid[rows_of(self.n), :] + p_in[rows_of(self.n), :]

    class Spread:
        def __init__(self, buf):
            self.buf = buf

        def piece(self, yy, hh, cols=None):
            rows = rows_of(hh * 4 + yy)
            return self.buf.at[rows] if cols is None else self.buf.at[rows, cols]

        def start(self):
            mine = self.piece(y, xh)
            self.x = rcopy(mine, mine, across)
            self.own = [rcopy(mine, mine, yp), rcopy(mine, mine, ym)]

        def second(self):
            self.x.wait_recv()
            other = self.piece(y, 1 - xh)
            self.oth = [rcopy(other, other, yp), rcopy(other, other, ym)]

        def forward(self, which):
            cps, hh = (self.own, xh) if which == 0 else (self.oth, 1 - xh)
            cps[0].wait_recv()
            p = self.piece((y + 3) % 4, hh, cols_of(0))
            f0 = rcopy(p, p, yp)
            cps[1].wait_recv()
            p = self.piece((y + 1) % 4, hh, cols_of(1))
            f1 = rcopy(p, p, ym)
            return [f0, f1]

    class ZReduce:
        def __init__(self, src, n):
            self.src, self.n = src, n

        def slot(self, off):
            return rows_of(self.n * 7 + (off + 3 if off < 4 else 0))

        def at(self, off):
            return rows_of(self.n * 8 + PLACE[off])

        def step1(self):
            lo, hi = cols_of(0), cols_of(1)
            z_send[self.at(4), :] = self.src[rows_of(PLACE[4]), :].astype(BF)
            self.plus = rcopy(z_send.at[self.at(4), lo], z_recv.at[self.at(3), lo], zp)
            self.minus = rcopy(z_send.at[self.at(4), hi], z_recv.at[self.at(-3), hi], zm)

        def step(self, off):
            lo, hi = cols_of(0), cols_of(1)
            for sign in (1, -1):
                o = off * sign
                s = rows_of(PLACE[o])
                if off == 3:
                    raw, add = (hi, lo) if sign > 0 else (lo, hi)
                    z_send[self.at(o), raw] = self.src[s, raw].astype(BF)
                    (self.plus if sign > 0 else self.minus).wait_recv()
                    z_send[self.at(o), add] = (
                        self.src[s, add] + z_recv[self.at(o), add].astype(F32)).astype(BF)
                else:
                    (self.plus if sign > 0 else self.minus).wait_recv()
                    z_send[self.at(o), :] = (
                        self.src[s, :] + z_recv[self.at(o), :].astype(F32)).astype(BF)
                to = 0 if off == 1 else o - sign
                dst = z_recv.at[self.at(to if off > 1 else (0 if sign > 0 else 4))]
                cp = rcopy(z_send.at[self.at(o)], dst, zp if sign > 0 else zm)
                if sign > 0:
                    self.plus = cp
                else:
                    self.minus = cp

        def finish(self, out):
            self.plus.wait_recv()
            self.minus.wait_recv()
            t = (self.src[rows_of(0), :] + z_recv[self.at(0), :].astype(F32)
                 + z_recv[self.at(4), :].astype(F32))
            n = self.n
            i, j, m = sem(), sem(), sem()
            f_send[rows_of(n), :] = t
            far = [pltpu.make_async_remote_copy(
                src_ref=f_send.at[rows_of(n), cols_of(q)], dst_ref=f_recv.at[rows_of(2 * n)],
                send_sem=ssem.at[(i, j)[q]], recv_sem=rsem.at[i],
                device_id=(other0, other1)[q], device_id_type=MESH) for q in (0, 1)]
            near = pltpu.make_async_remote_copy(
                src_ref=f_send.at[rows_of(n), cols_of(1 - k)], dst_ref=f_recv.at[rows_of(2 * n + 1)],
                send_sem=ssem.at[m], recv_sem=rsem.at[m], device_id=mate, device_id_type=MESH)

            @pl.when(xl != k)
            def _():
                far[0].start()
                far[1].start()

            @pl.when(xl == k)
            def _():
                near.start()

            def done():
                far[0].wait_recv()

                @pl.when(xl != k)
                def _():
                    near.wait_recv()
                    small[rows_of(n), :] = (
                        f_recv[rows_of(2 * n), :]
                        + f_recv[rows_of(2 * n + 1), :]).astype(BF)
                    far[0].wait_send()
                    far[1].wait_send()

                @pl.when(xl == k)
                def _():
                    small[rows_of(n), :] = (
                        f_recv[rows_of(2 * n), :]
                        + f_send[rows_of(n), cols_of(k)]).astype(BF)
                    near.wait_send()

                return lcopy(small.at[rows_of(n)], out)

            return done

    other_rows = pl.ds(ROWS, ROWS)
    half_rows = pl.ds(0, ROWS)

    def weight_grad(lhs_a, lhs_b, rhs, out, steps, own_off):
        def body(m, _):
            rows = pl.ds(pl.multiple_of(m * 128, 128), 128)
            cols = pl.ds(pl.multiple_of(m * 128 + own_off, 128), 128)
            dims = (((0,), (0,)), ((), ()))
            v = lax.dot_general(lhs_a[half_rows, cols], rhs[half_rows, :], dims, preferred_element_type=F32)
            v = v + lax.dot_general(lhs_b[:, rows], rhs[other_rows, :], dims, preferred_element_type=F32)
            out[rows, :] = v.astype(BF)
            return 0

        lax.fori_loop(0, steps, body, 0)

    gt, gg = Gather(tok, tok_arrived), Gather(grad, grad_arrived)
    gt.step(1)
    own_up.wait()
    w1.wait_recv()
    matmul(tok, up, part.at[0], PLACE[0], False)
    gt.step(2)
    for o in (1, -1):
        matmul(tok, up, part.at[0], PLACE[o], False)
    gt.step(3)
    own_down.wait()
    w2.wait_recv()
    red_p, red_q = Reduce(part.at[0], 0), Reduce(part.at[1], 1)
    for o in (2, -2):
        matmul(tok, up, part.at[0], PLACE[o], False)
    red_p.step1(0)
    gt.step(4)
    gg.step(1)
    for o in (3, -3):
        matmul(tok, up, part.at[0], PLACE[o], False)
    red_p.step2(0)
    gt.finish()
    matmul(tok, up, part.at[0], PLACE[4], False)
    red_p.step1(1)
    gg.step(2)
    matmul(grad, down, part.at[1], PLACE[0], True)
    red_p.step2(1)
    red_p.cross(0)
    for o in (1, -1):
        matmul(grad, down, part.at[1], PLACE[o], True)
    gg.step(3)
    red_p.cross(1)
    red_p.send()
    tok_mate = rcopy(tok.at[:, cols_of(1 - k)], tok_o, mate)
    for o in (2, -2):
        matmul(grad, down, part.at[1], PLACE[o], True)
    gg.step(4)
    red_q.step1(0)
    h = red_p.result()
    hid[rows_of(0), :] = h
    act[rows_of(xh * 4 + y), :] = gelu(h).astype(BF)
    sp_a = Spread(act)
    sp_a.start()
    for o in (3, -3):
        matmul(grad, down, part.at[1], PLACE[o], True)
    red_q.step2(0)
    gg.finish()
    matmul(grad, down, part.at[1], PLACE[4], True)
    sp_a.second()
    red_q.step1(1)
    grad_mate = rcopy(grad.at[:, cols_of(1 - k)], grad_o, mate)
    fa = sp_a.forward(0)
    red_q.step2(1)
    fa += sp_a.forward(1)
    red_q.cross(0)
    red_q.cross(1)
    red_q.send()
    for cp in fa:
        cp.wait_recv()
    act_mate = rcopy(act.at[half_rows], act.at[other_rows], mate)
    zm_ = ZReduce(part.at[0], 0)
    matmul(act, down, part.at[0], PLACE[4], False)
    zm_.step1()
    for o in (3, -3):
        matmul(act, down, part.at[0], PLACE[o], False)
    d = red_q.result()
    hgrad[rows_of(xh * 4 + y), :] = (d * gelu_slope(hid[rows_of(0), :])).astype(BF)
    sp_h = Spread(hgrad)
    sp_h.start()
    zm_.step(3)
    for o in (2, -2):
        matmul(act, down, part.at[0], PLACE[o], False)
    sp_h.second()
    zm_.step(2)
    fh = sp_h.forward(0)
    for o in (1, -1):
        matmul(act, down, part.at[0], PLACE[o], False)
    zm_.step(1)
    fh += sp_h.forward(1)
    matmul(act, down, part.at[0], PLACE[0], False)
    for cp in fh:
        cp.wait_recv()
    zi = ZReduce(part.at[1], 1)
    matmul(hgrad, up, part.at[1], PLACE[4], True)
    zi.step1()
    for o in (3, -3):
        matmul(hgrad, up, part.at[1], PLACE[o], True)
    hg_mate = rcopy(hgrad.at[half_rows], hgrad.at[other_rows], mate)
    done_m = zm_.finish(mixed_out)
    zi.step(3)
    for o in (2, -2):
        matmul(hgrad, up, part.at[1], PLACE[o], True)
    zi.step(2)
    for o in (1, -1):
        matmul(hgrad, up, part.at[1], PLACE[o], True)
    zi.step(1)
    matmul(hgrad, up, part.at[1], PLACE[0], True)
    out_m = done_m()
    tok_mate.wait_recv()
    hg_mate.wait_recv()
    weight_grad(tok, tok_o, hgrad, upg, HALF // 128, k * HALF)
    out_u = lcopy(upg, upg_out)
    done_i = zi.finish(igrad_out)
    grad_mate.wait_recv()
    act_mate.wait_recv()

    def down_body(m, _):
        rows = pl.ds(pl.multiple_of(m * 128, 128), 128)
        dims = (((0,), (0,)), ((), ()))
        v = lax.dot_general(act[half_rows, rows], grad[half_rows, cols_of(k)], dims, preferred_element_type=F32)
        v = v + lax.dot_general(act[other_rows, rows], grad_o[...], dims, preferred_element_type=F32)
        downg[rows, :] = v.astype(BF)
        return 0

    lax.fori_loop(0, WIDE // 128, down_body, 0)
    out_d = lcopy(downg, downg_out)
    out_i = done_i()
    for cp in sends:
        cp.wait_send()
    tok_sent()
    grad_sent()
    for cp in (out_m, out_u, out_d, out_i):
        cp.wait()


def local(tokens, up_weight, down_weight, grad_out):
    vm = pltpu.VMEM
    any_ = pl.BlockSpec(memory_space=pl.ANY)
    return pl.pallas_call(
        kernel,
        name="ffn",
        out_shape=(
            jax.ShapeDtypeStruct((TOK, HALF), BF),
            jax.ShapeDtypeStruct((TOK, HALF), BF),
            jax.ShapeDtypeStruct((HALF, WIDE), BF),
            jax.ShapeDtypeStruct((WIDE, HALF), BF),
        ),
        in_specs=[any_] * 4,
        out_specs=(any_,) * 4,
        scratch_shapes=[
            vm((WIDE, WIDE), BF), vm((WIDE, WIDE), BF),
            vm((ROWS, WIDE), BF), vm((ROWS, WIDE), BF),
            vm((2 * ROWS, WIDE), BF), vm((2 * ROWS, WIDE), BF),
            vm((ROWS, HALF), BF), vm((ROWS, HALF), BF),
            vm((2, ROWS, WIDE), F32),
            vm((2 * TOK, WIDE), F32),
            vm((12 * TOK, WIDE), BF), vm((12 * TOK, WIDE), BF),
            vm((2 * TOK, WIDE), F32), vm((2 * TOK, WIDE), F32),
            vm((16 * TOK, WIDE), BF), vm((16 * TOK, WIDE), BF),
            vm((2 * TOK, WIDE), F32), vm((4 * TOK, HALF), F32),
            vm((HALF, WIDE), BF), vm((WIDE, HALF), BF),
            vm((2 * TOK, HALF), BF),
            pltpu.SemaphoreType.DMA((128,)),
            pltpu.SemaphoreType.DMA((128,)),
            pltpu.SemaphoreType.DMA((16,)),
        ],
        compiler_params=pltpu.CompilerParams(
            collective_id=0, has_side_effects=True, vmem_limit_bytes=60 * 2**20
        ),
        cost_estimate=pl.CostEstimate(flops=12_600_000_000, bytes_accessed=10_000_000, transcendentals=300_000),
    )(tokens, up_weight, down_weight, grad_out)


def solution(mesh):
    placed = (P("col", "row"), P("row", "col"), P("col", "row"), P("col", "row"))
    return jax.shard_map(
        local,
        mesh=mesh,
        in_specs=placed,
        out_specs=(P("col", "row"), P("col", "row"), P("row", "col"), P("col", "row")),
        check_vma=False,
    )
```

```python
import jax
import jax.numpy as jnp
from jax import lax
from jax.experimental import pallas as pl
from jax.experimental.pallas import tpu as pltpu
from jax.sharding import PartitionSpec as P

MESH = pl.DeviceIdType.MESH
BF = jnp.bfloat16
F32 = jnp.float32

TOK = 80
HALF = 640
WIDE = 1280
ROWS = 8 * TOK

PLACE = {0: 0, 1: 1, -1: 2, 2: 3, -2: 4, 3: 5, -3: 6, 4: 7}
SPAN = ((0, 1), (1, 2), (3, 2), (5, 2), (7, 1))
SUB = ((0, 48), (48, 32))

C0 = 0.7978845608028654
C1 = 0.044715

ORDER = (
    "W2s", "W1s", "Gs", "Tzp0", "Tzm0", "D", "Tzp1", "Tzm1", "Q0", "Qx0", "Tzp2", "Tzm2",
    "P0", "Px0", "U", "Tzp3", "Tzm3", "P1", "Px2", "Tzp4", "Tzm4", "Px1", "Tzp5", "P2",
    "Tzm5", "Px4", "Tzp6", "Tzm6", "Px3", "Gzp0", "Gzm1", "P3", "Gzp1", "Px5", "Gzm0", "Px6",
    "P4", "Tm", "Py0pa", "Py0ma", "Gzp2", "Py0mb", "Py0pb", "Px7", "Gzm3", "Gzp3", "Gzm2", "Q1",
    "Py0mc", "Py0pc", "Qx1", "Gzp4", "Gzm5", "Qx2", "Gzp5", "Py1pa", "Py1ma", "Py1pb", "Gzm4", "Q2",
    "Pe0", "Gzp6", "Qx4", "Py1pc", "Py1mb", "Py1mc", "Gzm6", "Q3", "Qx5", "Pf0p", "Qx6", "Pn0",
    "Q4", "Pe1", "Gm", "Qx7", "Pf0m", "Qx3", "Pf1p", "Pn1", "M0", "M1", "Qy1ma", "Qy1pb",
    "Qy1mb", "Qy1pa", "Qy0ma", "Qy0pa", "Pf1m", "Qy0pb", "Qy1mc", "Qy1pc", "Qy0mc", "Qy0mb", "Qy0pc", "M4",
    "Mrp0", "Mrm0", "Qe1", "M3", "Mrp1", "Mrm1", "Qe0", "M2", "Am", "Mrp2", "Mrm2", "Qf1p",
    "Qn1", "Mrp3", "Mrm3", "Qn0", "Mrp4", "Mrm4", "DG0", "DG1", "Qf1m", "Qf0p", "Mrp5", "Mrm5",
    "DG2", "DG3", "Qf0m", "Mrp6", "Mrm6", "I4", "Irm0", "I3", "Irp1", "Irm1", "I2", "Irp0",
    "I1", "I0", "Hm", "Irm2", "Mt1", "Irp3", "Mt0", "Irm3", "Irp2", "Irm4", "UG0", "Irp5",
    "UG1", "Irp4", "Mo", "Irm5", "Irm6", "Irp6", "It1", "It0", "Io",
)


def gelu(v):
    return 0.5 * v * (1.0 + jnp.tanh(C0 * (v + C1 * v * v * v)))


def gelu_slope(v):
    t = jnp.tanh(C0 * (v + C1 * v * v * v))
    return 0.5 * (1.0 + t) + 0.5 * v * (1.0 - t * t) * (C0 * (1.0 + 3.0 * C1 * v * v))


def rows_of(place, many=1):
    if isinstance(place, int):
        return pl.ds(place * TOK, many * TOK)
    return pl.ds(pl.multiple_of(place * TOK, TOK), many * TOK)


def cols_of(half):
    if isinstance(half, int):
        return pl.ds(half * HALF, HALF)
    return pl.ds(pl.multiple_of(half * HALF, HALF), HALF)


def kernel(
    tok_in, up_in, down_in, grad_in,
    mixed_out, igrad_out, upg_out, downg_out,
    up, down, up_t, down_t, tok, grad, act, hgrad, tok_o, grad_o,
    part, hid, x_send, x_recv, y_send, y_recv, z_send, z_recv, f_send, f_recv,
    upg, downg, small,
    ssem, rsem, lsem,
):
    r, c = lax.axis_index("row"), lax.axis_index("col")
    y, xh, k = r // 4, (r // 2) % 2, r % 2
    xl, z = c // 8, c % 8

    def row_id(yy, hh, kk):
        return (yy * 2 + hh) * 2 + kk

    mate = (row_id(y, xh, 1 - k), c)
    yside = {"p": (row_id((y + 1) % 4, xh, k), c), "m": (row_id((y + 3) % 4, xh, k), c)}
    across = (row_id(y, 1 - xh, k), c)
    zside = {"p": (r, xl * 8 + (z + 1) % 8), "m": (r, xl * 8 + (z + 7) % 8)}
    other_c = (1 - xl) * 8 + z
    other = ((row_id(y, xh, 0), other_c), (row_id(y, xh, 1), other_c))

    count = [0, 0]
    ends = []
    msg = {}

    def sem():
        count[0] += 1
        return count[0] - 1

    def remote(src, dst, dev):
        i = sem()
        return pltpu.make_async_remote_copy(
            src_ref=src, dst_ref=dst, send_sem=ssem.at[i], recv_sem=rsem.at[i],
            device_id=dev, device_id_type=MESH,
        )

    def send(name, src, dst, dev):
        cp = remote(src, dst, dev)
        cp.start()
        ends.append(cp.wait_send)
        msg[name] = cp.wait_recv

    def got(*names):
        for name in names:
            wait = msg[name]
            if wait is not None:
                wait()
                msg[name] = None

    def lcopy(src, dst):
        cp = pltpu.make_async_copy(src, dst, lsem.at[count[1]])
        count[1] += 1
        cp.start()
        return cp.wait

    def unless(cond, f):
        def g():
            pl.when(cond)(f)

        return g

    own_rows = pl.ds(pl.multiple_of(k * HALF, HALF), HALF)
    msg["up"] = lcopy(up_in, up.at[own_rows])
    msg["down"] = lcopy(down_in, down.at[:, cols_of(k)])

    barrier = pltpu.get_barrier_semaphore()
    for dev in (mate, *yside.values(), across, *zside.values(), *other):
        pl.semaphore_signal(barrier, inc=1, device_id=dev, device_id_type=MESH)
    pl.semaphore_wait(barrier, 8)

    def spread(name, src, buf):
        i, j = sem(), sem()
        dst = buf.at[k, rows_of(0)]
        far = pltpu.make_async_remote_copy(
            src_ref=src, dst_ref=dst, send_sem=ssem.at[i], recv_sem=rsem.at[i + k],
            device_id=(row_id(y, xh, xl), other_c), device_id_type=MESH,
        )
        near = pltpu.make_async_remote_copy(
            src_ref=src, dst_ref=dst, send_sem=ssem.at[j], recv_sem=rsem.at[i + k],
            device_id=mate, device_id_type=MESH,
        )
        stay = pltpu.make_async_copy(src, dst, rsem.at[i + k])
        far.start()
        pl.when(k != xl)(near.start)
        pl.when(k == xl)(stay.start)
        ends.append(far.wait_send)
        ends.append(unless(k != xl, near.wait_send))
        for h in (0, 1):
            msg[f"{name}s{h}"] = pltpu.make_async_copy(src, buf.at[h, rows_of(0)], rsem.at[i + h]).wait

    spread("T", tok_in, tok)

    tasks = {}
    tasks["W1s"] = lambda: send("W1", up_in, up.at[own_rows], mate)
    tasks["W2s"] = lambda: send("W2", down_in, down.at[:, cols_of(k)], mate)
    tasks["Gs"] = lambda: spread("G", grad_in, grad)

    def gather(name, buf):
        def source(off, h):
            if off == 0:
                return f"{name}s{h}"
            if off == 4:
                return f"{name}zp6" if h == 0 else f"{name}zm6"
            d, first = ("p", 0) if off < 0 else ("m", 1)
            return f"{name}z{d}{2 * (abs(off) - 1) + (0 if h == first else 1)}"

        def step(d, i):
            n, first, sign = i // 2, 0 if d == "p" else 1, -1 if d == "p" else 1
            h = first if i % 2 == 0 else 1 - first
            off, to = sign * n, sign * (n + 1)
            got(source(off, h))
            send(f"{name}z{d}{i}", buf.at[h, rows_of(PLACE[off])],
                 buf.at[h, rows_of(PLACE[4 if to == -4 else to])], zside[d])

        for d in "pm":
            for i in range(7):
                tasks[f"{name}z{d}{i}"] = lambda d=d, i=i: step(d, i)
        return source

    tok_source, grad_source = gather("T", tok), gather("G", grad)

    def product(lhs, rhs, out, i):
        first, many = SPAN[i]
        rows = rows_of(first, many)
        v = (
            jnp.dot(lhs[0, rows, :], rhs[pl.ds(0, HALF), :], preferred_element_type=F32)
            + jnp.dot(lhs[1, rows, :], rhs[pl.ds(HALF, HALF), :], preferred_element_type=F32))
        out[0, rows, :] = v[:, :HALF]
        out[1, rows, :] = v[:, HALF:]

    def turn(src, dst):
        def body(n, _):
            cols = pl.ds(pl.multiple_of(n * 256, 256), 256)
            dst[:, cols] = src[cols, :].T
            return 0

        lax.fori_loop(0, WIDE // 256, body, 0)

    def turn_up():
        got("up", "W1")
        turn(up, up_t)

    def turn_down():
        got("down", "W2")
        turn(down, down_t)

    tasks["U"], tasks["D"] = turn_up, turn_down

    def offs(i):
        return (i,) if i in (0, 4) else (i, -i)

    def way(n, R, source, lhs, rhs, N, lhs2, rhs2, finish):
        src = part.at[n]

        def first(i):
            got("up", "W1", *(source(o, h) for o in offs(i) for h in (0, 1)))
            product(lhs, rhs, src, i)

        for i in range(5):
            tasks[f"{R}{i}"] = lambda i=i: first(i)

        def xbuf(p):
            return rows_of(n * 8 + p) if isinstance(p, int) else pl.ds(pl.multiple_of((n * 8 + p) * TOK, TOK), TOK)

        def xstep(p):
            x_send[xbuf(p), :] = src[1 - xh, rows_of(p), :].astype(BF)
            send(f"{R}x{p}", x_send.at[xbuf(p)], x_recv.at[xbuf(p)], across)

        def paired(p, r):
            start, many = SUB[r]
            rows = pl.ds(pl.multiple_of(p * TOK + start, 16), many)
            far = pl.ds(pl.multiple_of((n * 8 + p) * TOK + start, 16), many)
            return src[xh, rows, :] + x_recv[far, :].astype(F32)

        def ybuf(b, d, s, r):
            return pl.ds(((n * 2 + b) * 6 + "pm".index(d) * 3 + "abc".index(s)) * SUB[0][1], SUB[r][1])

        def ystep(b, d, s):
            got(*(f"{R}x{b * 4 + i}" for i in range(4)))
            near = 1 if d == "p" else 3
            r = b if d == "p" else 1 - b
            if s == "b":
                r = 1 - r
            v = paired(b * 4 + (y + (2 if s == "a" else near)) % 4, r)
            if s == "c":
                got(f"{R}y{b}{d}a")
                v = v + y_recv[ybuf(b, d, "a", r), :].astype(F32)
            mine = ybuf(b, d, s, r)
            y_send[mine, :] = v.astype(BF)
            send(f"{R}y{b}{d}{s}", y_send.at[mine], y_recv.at[mine], yside[d])

        def piece(b, yy, h):
            return lhs2.at[h, rows_of(b * 4 + yy)]

        def estep(b):
            got(*(f"{R}y{b}{d}{s}" for d in "pm" for s in "bc"))
            for r in (0, 1):
                p, m = ("c", "b") if r == b else ("b", "c")
                v = (paired(b * 4 + y, r) + y_recv[ybuf(b, "p", p, r), :].astype(F32)
                     + y_recv[ybuf(b, "m", m, r), :].astype(F32))
                start, many = SUB[r]
                v = finish(v, pl.ds(b * TOK + start, many)).astype(BF)
                lhs2[xh, pl.ds(pl.multiple_of((b * 4 + y) * TOK + start, 16), many), :] = v
            mine = piece(b, y, xh)
            for d in "pm":
                send(f"{R}o{b}{d}", mine, mine, yside[d])
            send(f"{R}a{b}", mine, mine, across)

        def nstep(b):
            got(f"{R}a{b}")
            theirs = piece(b, y, 1 - xh)
            for d in "pm":
                send(f"{R}n{b}{d}", theirs, theirs, yside[d])

        def fstep(b, d):
            if d == "p":
                got(f"{R}o{b}p")
                p = piece(b, (y + 3) % 4, xh)
            else:
                got(f"{R}n{b}m")
                p = piece(b, (y + 1) % 4, 1 - xh)
            send(f"{R}f{b}{d}", p, p, yside[d])

        for p in range(8):
            tasks[f"{R}x{p}"] = lambda p=p: xstep(p)
        for b in (0, 1):
            for d in "pm":
                for s in "abc":
                    tasks[f"{R}y{b}{d}{s}"] = lambda b=b, d=d, s=s: ystep(b, d, s)
                tasks[f"{R}f{b}{d}"] = lambda b=b, d=d: fstep(b, d)
            tasks[f"{R}e{b}"] = lambda b=b: estep(b)
            tasks[f"{R}n{b}"] = lambda b=b: nstep(b)

        def second(i):
            for b in {0: (0,), 1: (0,), 2: (0, 1), 3: (1,), 4: (1,)}[i]:
                got(*(f"{R}{q}{b}{d}" for q in "onf" for d in "pm"))
            got("down", "W2")
            product(lhs2, rhs2, src, i)

        for i in range(5):
            tasks[f"{N}{i}"] = lambda i=i: second(i)

        def zbuf(d, i):
            return rows_of(n * 14 + "pm".index(d) * 7 + i)

        def zstep(d, i):
            first = 0 if d == "p" else 1
            h = first if i % 2 == 0 else 1 - first
            o = 4 - (i + 1) // 2
            place = PLACE[o if d == "p" or o == 4 else -o]
            v = src[h, rows_of(place), :]
            if i >= 2:
                got(f"{N}r{d}{i - 2}")
                v = v + z_recv[zbuf(d, i - 2), :].astype(F32)
            z_send[zbuf(d, i), :] = v.astype(BF)
            send(f"{N}r{d}{i}", z_send.at[zbuf(d, i)], z_recv.at[zbuf(d, i)], zside[d])

        for d in "pm":
            for i in range(7):
                tasks[f"{N}r{d}{i}"] = lambda d=d, i=i: zstep(d, i)

        def tstep(h):
            p, m = (6, 5) if h == 0 else (5, 6)
            got(f"{N}rp{p}", f"{N}rm{m}")
            mine = rows_of(n * 2 + h)
            f_send[mine, :] = (src[h, rows_of(0), :] + z_recv[zbuf("p", p), :].astype(F32)
                               + z_recv[zbuf("m", m), :].astype(F32))
            if f"{N}far" not in msg:
                msg[f"{N}far"], msg[f"{N}near"] = sem(), sem()
            i, j = msg[f"{N}far"], msg[f"{N}near"]
            far = pltpu.make_async_remote_copy(
                src_ref=f_send.at[mine], dst_ref=f_recv.at[rows_of(2 * n)],
                send_sem=ssem.at[i if h == 0 else sem()], recv_sem=rsem.at[i],
                device_id=other[h], device_id_type=MESH)
            near = pltpu.make_async_remote_copy(
                src_ref=f_send.at[mine], dst_ref=f_recv.at[rows_of(2 * n + 1)],
                send_sem=ssem.at[j], recv_sem=rsem.at[j], device_id=mate, device_id_type=MESH)
            pl.when(xl != k)(far.start)
            give = jnp.logical_and(xl == k, k != h)
            pl.when(give)(near.start)
            ends.append(unless(xl != k, far.wait_send))
            ends.append(unless(give, near.wait_send))
            msg[f"{N}o"] = (far.wait_recv, near.wait_recv)

        def ostep():
            far, near = msg[f"{N}o"]
            far()
            mine = rows_of(n)

            @pl.when(xl != k)
            def _():
                near()
                small[mine, :] = (f_recv[rows_of(2 * n), :] + f_recv[rows_of(2 * n + 1), :]).astype(BF)

            @pl.when(xl == k)
            def _():
                small[mine, :] = (f_recv[rows_of(2 * n), :] + f_send[rows_of(n * 2 + k), :]).astype(BF)

            ends.append(lcopy(small.at[mine], (mixed_out, igrad_out)[n]))

        tasks[f"{N}t0"], tasks[f"{N}t1"], tasks[f"{N}o"] = lambda: tstep(0), lambda: tstep(1), ostep

    def forward(v, rows):
        hid[rows, :] = v
        return gelu(v)

    def backward(v, rows):
        return v * gelu_slope(hid[rows, :])

    way(0, "P", tok_source, tok, up, "M", act, down, forward)
    way(1, "Q", grad_source, grad, down_t, "I", hgrad, up_t, backward)

    low, high = pl.ds(0, ROWS), pl.ds(ROWS, ROWS)

    def swap(name, source, buf, out):
        got(*(source(o, h) for o in PLACE for h in (0, 1)))
        send(name, buf.at[1 - k], out, mate)

    tasks["Tm"] = lambda: swap("Tm", tok_source, tok, tok_o)
    tasks["Gm"] = lambda: swap("Gm", grad_source, grad, grad_o)

    def twin(name, buf):
        for h in (0, 1):
            send(f"{name}{h}", buf.at[h, low], buf.at[h, high], mate)

    tasks["Am"] = lambda: twin("Am", act)
    tasks["Hm"] = lambda: twin("Hm", hgrad)

    def outer(a, b):
        return lax.dot_general(a, b, (((0,), (0,)), ((), ())), preferred_element_type=F32)

    def dg(i):
        got("Gm", "Am0", "Am1")
        for h, first, many in (((0, 0, 256),), ((0, 256, 384),), ((1, 0, 256),), ((1, 256, 384),))[i]:
            cols, rows = pl.ds(first, many), pl.ds(h * HALF + first, many)
            v = outer(act[h, low, cols], grad[k]) + outer(act[h, high, cols], grad_o[...])
            downg[rows, :] = v.astype(BF)
            ends.append(lcopy(downg.at[rows], downg_out.at[rows]))

    def ug(i):
        got("Tm", "Hm0", "Hm1")
        rows = pl.ds(*((0, 256), (256, 384))[i])
        for h in (0, 1):
            v = outer(tok[k, :, rows], hgrad[h, low, :]) + outer(tok_o[:, rows], hgrad[h, high, :])
            upg[rows, cols_of(h)] = v.astype(BF)
        ends.append(lcopy(upg.at[rows], upg_out.at[rows]))

    for i in range(4):
        tasks[f"DG{i}"] = lambda i=i: dg(i)
    for i in range(2):
        tasks[f"UG{i}"] = lambda i=i: ug(i)

    for name in ORDER[:-1]:
        tasks[name]()
    for end in ends:
        end()
    ends.clear()
    tasks[ORDER[-1]]()
    for end in ends:
        end()


CUTS = 4


def hand_on(a, b, c, d, a_out, b_out, c_out, d_out, a_mid, b_mid, c_mid, d_mid, in_sem, out_sem):
    ins, outs = [], []
    for src, mid, dst, many in ((c, c_mid, c_out, CUTS), (d, d_mid, d_out, CUTS), (a, a_mid, a_out, 1), (b, b_mid, b_out, 1)):
        rows = src.shape[0] // many
        for i in range(many):
            part = pl.ds(i * rows, rows)
            n = len(ins)
            ins.append(pltpu.make_async_copy(src.at[part], mid.at[part], in_sem.at[n]))
            outs.append(pltpu.make_async_copy(mid.at[part], dst.at[part], out_sem.at[n]))
            ins[n].start()
    for first, then in zip(ins, outs):
        first.wait()
        then.start()
    for cp in outs:
        cp.wait()


def local(tokens, up_weight, down_weight, grad_out):
    vm = pltpu.VMEM
    any_ = pl.BlockSpec(memory_space=pl.ANY)
    done = pl.pallas_call(
        kernel,
        name="ffn",
        out_shape=(
            jax.ShapeDtypeStruct((TOK, HALF), BF),
            jax.ShapeDtypeStruct((TOK, HALF), BF),
            jax.ShapeDtypeStruct((HALF, WIDE), BF),
            jax.ShapeDtypeStruct((WIDE, HALF), BF),
        ),
        in_specs=[any_] * 4,
        out_specs=(any_,) * 4,
        scratch_shapes=[
            vm((WIDE, WIDE), BF), vm((WIDE, WIDE), BF),
            vm((WIDE, WIDE), BF), vm((WIDE, WIDE), BF),
            vm((2, ROWS, HALF), BF), vm((2, ROWS, HALF), BF),
            vm((2, 2 * ROWS, HALF), BF), vm((2, 2 * ROWS, HALF), BF),
            vm((ROWS, HALF), BF), vm((ROWS, HALF), BF),
            vm((2, 2, ROWS, HALF), F32),
            vm((2 * TOK, HALF), F32),
            vm((16 * TOK, HALF), BF), vm((16 * TOK, HALF), BF),
            vm((24 * 48, HALF), BF), vm((24 * 48, HALF), BF),
            vm((28 * TOK, HALF), BF), vm((28 * TOK, HALF), BF),
            vm((4 * TOK, HALF), F32), vm((4 * TOK, HALF), F32),
            vm((HALF, WIDE), BF), vm((WIDE, HALF), BF),
            vm((2 * TOK, HALF), BF),
            pltpu.SemaphoreType.DMA((160,)),
            pltpu.SemaphoreType.DMA((160,)),
            pltpu.SemaphoreType.DMA((16,)),
        ],
        compiler_params=pltpu.CompilerParams(
            collective_id=0, has_side_effects=True, vmem_limit_bytes=60 * 2**20
        ),
        cost_estimate=pl.CostEstimate(flops=12_600_000_000, bytes_accessed=10_000_000, transcendentals=300_000),
    )(tokens, up_weight, down_weight, grad_out)
    return pl.pallas_call(
        hand_on,
        name="hand_on",
        out_shape=[jax.ShapeDtypeStruct(x.shape, x.dtype) for x in done],
        in_specs=[any_] * 4,
        out_specs=[any_] * 4,
        scratch_shapes=[pltpu.VMEM(x.shape, x.dtype) for x in done]
        + [pltpu.SemaphoreType.DMA((2 * CUTS + 2,))] * 2,
        cost_estimate=pl.CostEstimate(flops=0, bytes_accessed=8_000_000, transcendentals=0),
    )(*done)


def solution(mesh):
    placed = (P("col", "row"), P("row", "col"), P("col", "row"), P("col", "row"))
    return jax.shard_map(
        local,
        mesh=mesh,
        in_specs=placed,
        out_specs=(P("col", "row"), P("col", "row"), P("row", "col"), P("col", "row")),
        check_vma=False,
    )
```

```python
import jax
import jax.numpy as jnp
from jax import lax
from jax.experimental import pallas as pl
from jax.experimental.pallas import tpu as pltpu
from jax.sharding import PartitionSpec as P

MESH = pl.DeviceIdType.MESH
BF = jnp.bfloat16
F32 = jnp.float32

TOK = 80
HALF = 640
WIDE = 1280
ROWS = 8 * TOK

PLACE = {0: 0, 1: 1, -1: 2, 2: 3, -2: 4, 3: 5, -3: 6, 4: 7}
SPAN = ((0, 1), (1, 2), (3, 2), (5, 2), (7, 1))
SUB = ((0, 48), (48, 32))

C0 = 0.7978845608028654
C1 = 0.044715

ORDER = (
    "Gs", "W1s", "W2s", "Tzp2", "Tzm2", "P1", "Tzm3", "Gzm2", "Tzp3", "P0", "D", "Gzp3",
    "Tzp4", "Tzm4", "Gzm3", "Gzp2", "Q1", "Tzp5", "P2", "Qx2", "Py0pa", "Py0ma", "Qx1", "Tzm5",
    "Py0pb", "Tzp6", "Tzm6", "Q0", "Py0mb", "Qx0", "Gzm4", "Gzp4", "Gzp5", "Q2", "Py0pc", "Py0mc",
    "Gzm5", "Qx4", "P3", "Qx3", "P4", "Py1pa", "Gzm6", "Py1ma", "Gzp6", "Py1pb", "Px01", "Py1mb",
    "Q3", "Qx6", "Py1pc", "Qx5", "Py1mc", "Qy0pa", "Q4", "Qy0ma", "Qx7", "Pe01", "Px10", "Qy0mb",
    "Gm", "Qy0mc", "Px11", "Qy0pc", "Qy0pb", "Qy1mb", "Qy1pb", "Qy1ma", "Px00", "Qy1pa", "Pe10", "Pe11",
    "Qy1pc", "Qy1mc", "U", "Tm", "Pf1p", "Pf1m", "Pf0m", "Pe00", "Qe1", "M4", "Mrp0", "Mrm0",
    "Pf0p", "M3", "Mrp1", "Mrm1", "Qn1", "Qe0", "Qf1p", "Mrp2", "Mrm2", "M2", "Mrp3", "Mrm3",
    "Qf1m", "Am", "Qn0", "Mrp4", "Mrm4", "M1", "Mrp5", "Mrm5", "I4", "Irp0", "Irm0", "Qf0p",
    "I3", "Qf0m", "Irm1", "Irp1", "M0", "DG3", "Irp2", "Irm2", "Mrp6", "I2", "Irm3", "I1",
    "Mw", "Irp4", "Irm4", "I0", "Irp3", "Mrm6", "DG1", "Hm", "Iw", "Irm5", "Irp6", "DG0",
    "Irm6", "Irp5", "Mt0", "Mt1", "DG2", "UG0", "Mo", "It0", "It1", "UG1", "Io",
)


def gelu(v):
    return 0.5 * v * (1.0 + jnp.tanh(C0 * (v + C1 * v * v * v)))


def gelu_slope(v):
    t = jnp.tanh(C0 * (v + C1 * v * v * v))
    return 0.5 * (1.0 + t) + 0.5 * v * (1.0 - t * t) * (C0 * (1.0 + 3.0 * C1 * v * v))


def rows_of(place, many=1):
    if isinstance(place, int):
        return pl.ds(place * TOK, many * TOK)
    return pl.ds(pl.multiple_of(place * TOK, TOK), many * TOK)


def cols_of(half):
    if isinstance(half, int):
        return pl.ds(half * HALF, HALF)
    return pl.ds(pl.multiple_of(half * HALF, HALF), HALF)


def kernel(
    tok_in, up_in, down_in, grad_in,
    mixed_out, igrad_out, upg_out, downg_out,
    up, down, up_t, down_t, tok, grad, act, hgrad, tok_o, grad_o,
    part, hid, h_send, h_recv, x_send, x_recv, y_send, y_recv, z_send, z_recv, s_recv, w_send, w_recv, f_send, f_recv,
    upg, downg, small,
    ssem, rsem, lsem,
):
    r, c = lax.axis_index("row"), lax.axis_index("col")
    y, xh, k = r // 4, (r // 2) % 2, r % 2
    xl, z = c // 8, c % 8

    def row_id(yy, hh, kk):
        return (yy * 2 + hh) * 2 + kk

    mate = (row_id(y, xh, 1 - k), c)
    yside = {"p": (row_id((y + 1) % 4, xh, k), c), "m": (row_id((y + 3) % 4, xh, k), c)}
    across = (row_id(y, 1 - xh, k), c)
    zside = {"p": (r, xl * 8 + (z + 1) % 8), "m": (r, xl * 8 + (z + 7) % 8)}
    other_c = (1 - xl) * 8 + z
    other = ((row_id(y, xh, 0), other_c), (row_id(y, xh, 1), other_c))
    zstep_of = {"p": (z + 1) % 8, "m": (z + 7) % 8}
    slant = {d: (r, (1 - xl) * 8 + zstep_of[d]) for d in "pm"}
    givers = [(row_id(y, xh, q), k * 8 + zstep_of[d]) for d in "pm" for q in (0, 1)]

    count = [0, 0]
    ends = []
    msg = {}

    def sem():
        count[0] += 1
        return count[0] - 1

    def remote(src, dst, dev):
        i = sem()
        return pltpu.make_async_remote_copy(
            src_ref=src, dst_ref=dst, send_sem=ssem.at[i], recv_sem=rsem.at[i],
            device_id=dev, device_id_type=MESH,
        )

    def send(name, src, dst, dev):
        cp = remote(src, dst, dev)
        cp.start()
        ends.append(cp.wait_send)
        msg[name] = cp.wait_recv

    def got(*names):
        for name in names:
            wait = msg[name]
            if wait is not None:
                wait()
                msg[name] = None

    def lcopy(src, dst):
        cp = pltpu.make_async_copy(src, dst, lsem.at[count[1]])
        count[1] += 1
        cp.start()
        return cp.wait

    def unless(cond, f):
        def g():
            pl.when(cond)(f)

        return g

    own_rows = pl.ds(pl.multiple_of(k * HALF, HALF), HALF)
    msg["up"] = lcopy(up_in, up.at[own_rows])
    msg["down"] = lcopy(down_in, down.at[:, cols_of(k)])

    barrier = pltpu.get_barrier_semaphore()
    for dev in (mate, *yside.values(), across, *zside.values(), *other, *slant.values(), *givers):
        pl.semaphore_signal(barrier, inc=1, device_id=dev, device_id_type=MESH)
    pl.semaphore_wait(barrier, 14)

    def spread(name, src, buf):
        def to(place, col, core, i):
            j = sem()
            cp = pltpu.make_async_remote_copy(
                src_ref=src, dst_ref=buf.at[k, rows_of(place)], send_sem=ssem.at[j], recv_sem=rsem.at[i + k],
                device_id=(core, col), device_id_type=MESH,
            )
            return cp

        def arrived(place, i, h):
            return pltpu.make_async_copy(src, buf.at[h, rows_of(place)], rsem.at[i + h]).wait

        target = row_id(y, xh, xl)
        for straight in (True, False):
            for d in "pm":
                place = PLACE[-1 if d == "p" else 1]
                if straight:
                    msg[name + d] = sem(), sem()
                i = msg[name + d][0]
                cp = to(place, (xl if straight else 1 - xl) * 8 + zstep_of[d], target, i)
                cp.start()
                ends.append(cp.wait_send)
                if not straight:
                    for h in (0, 1):
                        msg[f"{name}z{d}{h if d == 'p' else 1 - h}"] = arrived(place, i, h)
        i, _ = sem(), sem()
        far = to(0, other_c, target, i)
        near = to(0, c, row_id(y, xh, 1 - k), i)
        stay = pltpu.make_async_copy(src, buf.at[k, rows_of(0)], rsem.at[i + k])
        far.start()
        pl.when(k != xl)(near.start)
        pl.when(k == xl)(stay.start)
        ends.append(far.wait_send)
        ends.append(unless(k != xl, near.wait_send))
        for h in (0, 1):
            msg[f"{name}s{h}"] = arrived(0, i, h)

    spread("T", tok_in, tok)

    tasks = {}
    tasks["W1s"] = lambda: send("W1", up_in, up.at[own_rows], mate)
    tasks["W2s"] = lambda: send("W2", down_in, down.at[:, cols_of(k)], mate)
    tasks["Gs"] = lambda: spread("G", grad_in, grad)

    def gather(name, buf):
        def source(off, h):
            if off == 0:
                return f"{name}s{h}"
            if off == 4:
                return f"{name}zp6" if h == 0 else f"{name}zm6"
            d, first = ("p", 0) if off < 0 else ("m", 1)
            return f"{name}z{d}{2 * (abs(off) - 1) + (0 if h == first else 1)}"

        def step(d, i):
            n, first, sign = i // 2, 0 if d == "p" else 1, -1 if d == "p" else 1
            h = first if i % 2 == 0 else 1 - first
            off, to = sign * n, sign * (n + 1)
            got(source(off, h))
            send(f"{name}z{d}{i}", buf.at[h, rows_of(PLACE[off])],
                 buf.at[h, rows_of(PLACE[4 if to == -4 else to])], zside[d])

        for d in "pm":
            for i in range(2, 7):
                tasks[f"{name}z{d}{i}"] = lambda d=d, i=i: step(d, i)
        return source

    tok_source, grad_source = gather("T", tok), gather("G", grad)

    def product(lhs, rhs, out, i):
        first, many = SPAN[i]
        rows = rows_of(first, many)
        v = (
            jnp.dot(lhs[0, rows, :], rhs[pl.ds(0, HALF), :], preferred_element_type=F32)
            + jnp.dot(lhs[1, rows, :], rhs[pl.ds(HALF, HALF), :], preferred_element_type=F32))
        out[0, rows, :] = v[:, :HALF]
        out[1, rows, :] = v[:, HALF:]

    def turn(src, dst):
        def body(n, _):
            cols = pl.ds(pl.multiple_of(n * 256, 256), 256)
            dst[:, cols] = src[cols, :].T
            return 0

        lax.fori_loop(0, WIDE // 256, body, 0)

    def turn_up():
        got("up", "W1")
        turn(up, up_t)

    def turn_down():
        got("down", "W2")
        turn(down, down_t)

    tasks["U"], tasks["D"] = turn_up, turn_down

    def offs(i):
        return (i,) if i in (0, 4) else (i, -i)

    def way(n, R, source, lhs, rhs, N, lhs2, rhs2, finish):
        src = part.at[n]

        def first(i):
            got("up", "W1", *(source(o, h) for o in offs(i) for h in (0, 1)))
            product(lhs, rhs, src, i)

        for i in range(5):
            tasks[f"{R}{i}"] = lambda i=i: first(i)

        def fbuf(b, d, s):
            return rows_of(b * 6 + "pm".index(d) * 3 + "abc".index(s))

        def ywhole(b, d, s):
            near = 1 if d == "p" else 3
            h = 0 if d == "p" else 1
            if s == "b":
                h = 1 - h
            v = src[h, rows_of(b * 4 + (y + (2 if s == "a" else near)) % 4), :]
            if s == "c":
                got(f"{R}y{b}{d}a")
                v = v + y_recv[fbuf(b, d, "a"), :].astype(F32)
            mine = fbuf(b, d, s)
            y_send[mine, :] = v.astype(BF)
            send(f"{R}y{b}{d}{s}", y_send.at[mine], y_recv.at[mine], yside[d])

        def xwhole(b, h):
            p, m = ("c", "b") if h == 0 else ("b", "c")
            got(f"{R}y{b}p{p}", f"{R}y{b}m{m}")
            rows = rows_of(b * 2 + h)
            t = (src[h, rows_of(b * 4 + y), :] + y_recv[fbuf(b, "p", p), :].astype(F32)
                 + y_recv[fbuf(b, "m", m), :].astype(F32))
            hid[rows, :] = t
            h_send[rows, :] = t.astype(BF)
            send(f"{R}x{b}{h}", h_send.at[rows], h_recv.at[rows], across)

        def ewhole(b, h):
            got(f"{R}x{b}{h}")
            rows = rows_of(b * 2 + h)
            mine = lhs2.at[h, rows_of(b * 4 + y)]
            mine[...] = finish(hid[rows, :] + h_recv[rows, :].astype(F32), rows).astype(BF)
            for d in "pm":
                send(f"{R}o{b}{h}{d}", mine, mine, yside[d])

        def fwhole(b, d):
            h, yy = (0, (y + 3) % 4) if d == "p" else (1, (y + 1) % 4)
            got(f"{R}o{b}{h}{d}")
            p = lhs2.at[h, rows_of(b * 4 + yy)]
            send(f"{R}f{b}{d}", p, p, yside[d])

        for b in (0, 1) if n == 0 else ():
            for d in "pm":
                for s in "abc":
                    tasks[f"{R}y{b}{d}{s}"] = lambda b=b, d=d, s=s: ywhole(b, d, s)
                tasks[f"{R}f{b}{d}"] = lambda b=b, d=d: fwhole(b, d)
            for h in (0, 1):
                tasks[f"{R}x{b}{h}"] = lambda b=b, h=h: xwhole(b, h)
                tasks[f"{R}e{b}{h}"] = lambda b=b, h=h: ewhole(b, h)

        def xbuf(p):
            return rows_of(p)

        def xstep(p):
            x_send[xbuf(p), :] = src[1 - xh, rows_of(p), :].astype(BF)
            send(f"{R}x{p}", x_send.at[xbuf(p)], x_recv.at[xbuf(p)], across)

        def paired(p, r):
            start, many = SUB[r]
            rows = pl.ds(pl.multiple_of(p * TOK + start, 16), many)
            far = pl.ds(pl.multiple_of(p * TOK + start, 16), many)
            return src[xh, rows, :] + x_recv[far, :].astype(F32)

        def ybuf(b, d, s, r):
            return pl.ds(12 * TOK + (b * 6 + "pm".index(d) * 3 + "abc".index(s)) * SUB[0][1], SUB[r][1])

        def ystep(b, d, s):
            got(*(f"{R}x{b * 4 + i}" for i in range(4)))
            near = 1 if d == "p" else 3
            r = b if d == "p" else 1 - b
            if s == "b":
                r = 1 - r
            v = paired(b * 4 + (y + (2 if s == "a" else near)) % 4, r)
            if s == "c":
                got(f"{R}y{b}{d}a")
                v = v + y_recv[ybuf(b, d, "a", r), :].astype(F32)
            mine = ybuf(b, d, s, r)
            y_send[mine, :] = v.astype(BF)
            send(f"{R}y{b}{d}{s}", y_send.at[mine], y_recv.at[mine], yside[d])

        def piece(b, yy, h):
            return lhs2.at[h, rows_of(b * 4 + yy)]

        def estep(b):
            got(*(f"{R}y{b}{d}{s}" for d in "pm" for s in "bc"))
            for r in (0, 1):
                p, m = ("c", "b") if r == b else ("b", "c")
                v = (paired(b * 4 + y, r) + y_recv[ybuf(b, "p", p, r), :].astype(F32)
                     + y_recv[ybuf(b, "m", m, r), :].astype(F32))
                start, many = SUB[r]
                v = finish(v, pl.ds(pl.multiple_of((b * 2 + xh) * TOK + start, 16), many)).astype(BF)
                lhs2[xh, pl.ds(pl.multiple_of((b * 4 + y) * TOK + start, 16), many), :] = v
            mine = piece(b, y, xh)
            for d in "pm":
                send(f"{R}o{b}{d}", mine, mine, yside[d])
            send(f"{R}a{b}", mine, mine, across)

        def nstep(b):
            got(f"{R}a{b}")
            theirs = piece(b, y, 1 - xh)
            for d in "pm":
                send(f"{R}n{b}{d}", theirs, theirs, yside[d])

        def fstep(b, d):
            if d == "p":
                got(f"{R}o{b}p")
                p = piece(b, (y + 3) % 4, xh)
            else:
                got(f"{R}n{b}m")
                p = piece(b, (y + 1) % 4, 1 - xh)
            send(f"{R}f{b}{d}", p, p, yside[d])

        for p in range(8 if n == 1 else 0):
            tasks[f"{R}x{p}"] = lambda p=p: xstep(p)
        for b in (0, 1) if n == 1 else ():
            for d in "pm":
                for s in "abc":
                    tasks[f"{R}y{b}{d}{s}"] = lambda b=b, d=d, s=s: ystep(b, d, s)
                tasks[f"{R}f{b}{d}"] = lambda b=b, d=d: fstep(b, d)
            tasks[f"{R}e{b}"] = lambda b=b: estep(b)
            tasks[f"{R}n{b}"] = lambda b=b: nstep(b)

        def second(i):
            for b in {0: (0,), 1: (0,), 2: (0, 1), 3: (1,), 4: (1,)}[i]:
                got(*(f"{R}{q}{b}{d}" for q in "fon" for d in "pm" if f"{R}{q}{b}{d}" in msg),
                    *(f"{R}o{b}{h}{d}" for h in (0, 1) for d in "pm" if f"{R}o{b}{h}{d}" in msg))
            got("down", "W2")
            product(lhs2, rhs2, src, i)

        for i in range(5):
            tasks[f"{N}{i}"] = lambda i=i: second(i)

        def zbuf(d, i):
            return rows_of(n * 14 + "pm".index(d) * 7 + i)

        def zstep(d, i):
            first = 0 if d == "p" else 1
            h = first if i % 2 == 0 else 1 - first
            o = 4 - (i + 1) // 2
            place = PLACE[o if d == "p" or o == 4 else -o]
            v = src[h, rows_of(place), :]
            if i >= 2:
                got(f"{N}r{d}{i - 2}")
                v = v + z_recv[zbuf(d, i - 2), :].astype(F32)
            z_send[zbuf(d, i), :] = v.astype(BF)
            if i < 5:
                send(f"{N}r{d}{i}", z_send.at[zbuf(d, i)], z_recv.at[zbuf(d, i)], zside[d])
                return
            there = rows_of(n * 4 + "pm".index(d) * 2 + i - 5)
            straight = remote(z_send.at[zbuf(d, i)], z_recv.at[zbuf(d, i)], zside[d])
            aslant = remote(z_send.at[zbuf(d, i)], s_recv.at[there], slant[d])
            pl.when(xl == k)(straight.start)
            pl.when(xl != k)(aslant.start)
            ends.append(unless(xl == k, straight.wait_send))
            ends.append(unless(xl != k, aslant.wait_send))
            msg[f"{N}r{d}{i}"] = straight.wait_recv
            msg[f"{N}s{d}{i}"] = aslant.wait_recv

        for d in "pm":
            for i in range(7):
                tasks[f"{N}r{d}{i}"] = lambda d=d, i=i: zstep(d, i)

        def wstep():
            cps = []
            for h in (0, 1):
                mine = rows_of(n * 2 + h)
                cps.append(remote(w_send.at[mine], w_recv.at[mine], (r, other_c)))

            @pl.when(xl != k)
            def _():
                for h in (0, 1):
                    w_send[rows_of(n * 2 + h), :] = src[h, rows_of(0), :].astype(BF)
                for cp in cps:
                    cp.start()

            for h, cp in enumerate(cps):
                ends.append(unless(xl != k, cp.wait_send))
                msg[f"{N}w{h}"] = cp.wait_recv

        def tstep(h):
            mine = rows_of(n * 2 + h)
            cp = remote(f_send.at[mine], f_recv.at[rows_of(n)], mate)

            @pl.when(xl == k)
            def _():
                v = src[h, rows_of(0), :]
                msg[f"{N}w{h}"]()
                v = v + w_recv[mine, :].astype(F32)
                for d in "pm":
                    i = 6 if (h == 0) == (d == "p") else 5
                    msg[f"{N}r{d}{i}"]()
                    msg[f"{N}s{d}{i}"]()
                    there = rows_of(n * 4 + "pm".index(d) * 2 + i - 5)
                    v = v + z_recv[zbuf(d, i), :].astype(F32) + s_recv[there, :].astype(F32)
                f_send[mine, :] = v
                pl.when(k != h)(cp.start)

            give = jnp.logical_and(xl == k, k != h)
            ends.append(unless(give, cp.wait_send))
            msg[f"{N}t{h}"] = unless(jnp.logical_and(xl != k, k == h), cp.wait_recv)

        def ostep():
            mine = rows_of(n)
            msg[f"{N}t0"]()
            msg[f"{N}t1"]()

            @pl.when(xl != k)
            def _():
                small[mine, :] = f_recv[mine, :].astype(BF)

            @pl.when(xl == k)
            def _():
                small[mine, :] = f_send[rows_of(n * 2 + k), :].astype(BF)

            ends.append(lcopy(small.at[mine], (mixed_out, igrad_out)[n]))

        tasks[f"{N}w"] = wstep
        tasks[f"{N}t0"], tasks[f"{N}t1"], tasks[f"{N}o"] = lambda: tstep(0), lambda: tstep(1), ostep

    def forward(v, rows):
        hid[rows, :] = v
        return gelu(v)

    def backward(v, rows):
        return v * gelu_slope(hid[rows, :])

    way(0, "P", tok_source, tok, up, "M", act, down, forward)
    way(1, "Q", grad_source, grad, down_t, "I", hgrad, up_t, backward)

    low, high = pl.ds(0, ROWS), pl.ds(ROWS, ROWS)

    def swap(name, source, buf, out):
        got(*(source(o, h) for o in PLACE for h in (0, 1)))
        send(name, buf.at[1 - k], out, mate)

    tasks["Tm"] = lambda: swap("Tm", tok_source, tok, tok_o)
    tasks["Gm"] = lambda: swap("Gm", grad_source, grad, grad_o)

    def twin(name, buf):
        for h in (0, 1):
            send(f"{name}{h}", buf.at[h, low], buf.at[h, high], mate)

    tasks["Am"] = lambda: twin("Am", act)
    tasks["Hm"] = lambda: twin("Hm", hgrad)

    def outer(a, b):
        return lax.dot_general(a, b, (((0,), (0,)), ((), ())), preferred_element_type=F32)

    def dg(i):
        got("Gm", "Am0", "Am1")
        for h, first, many in (((0, 0, 256),), ((0, 256, 384),), ((1, 0, 256),), ((1, 256, 384),))[i]:
            cols, rows = pl.ds(first, many), pl.ds(h * HALF + first, many)
            v = outer(act[h, low, cols], grad[k]) + outer(act[h, high, cols], grad_o[...])
            downg[rows, :] = v.astype(BF)
            ends.append(lcopy(downg.at[rows], downg_out.at[rows]))

    def ug(i):
        got("Tm", "Hm0", "Hm1")
        rows = pl.ds(*((0, 256), (256, 384))[i])
        for h in (0, 1):
            v = outer(tok[k, :, rows], hgrad[h, low, :]) + outer(tok_o[:, rows], hgrad[h, high, :])
            upg[rows, cols_of(h)] = v.astype(BF)
        ends.append(lcopy(upg.at[rows], upg_out.at[rows]))

    for i in range(4):
        tasks[f"DG{i}"] = lambda i=i: dg(i)
    for i in range(2):
        tasks[f"UG{i}"] = lambda i=i: ug(i)

    for name in ORDER[:-1]:
        tasks[name]()
    for end in ends:
        end()
    ends.clear()
    tasks[ORDER[-1]]()
    for end in ends:
        end()


CUTS = 4


def hand_on(a, b, c, d, a_out, b_out, c_out, d_out, a_mid, b_mid, c_mid, d_mid, in_sem, out_sem):
    ins, outs = [], []
    for src, mid, dst, many in ((c, c_mid, c_out, CUTS), (d, d_mid, d_out, CUTS), (a, a_mid, a_out, 1), (b, b_mid, b_out, 1)):
        rows = src.shape[0] // many
        for i in range(many):
            part = pl.ds(i * rows, rows)
            n = len(ins)
            ins.append(pltpu.make_async_copy(src.at[part], mid.at[part], in_sem.at[n]))
            outs.append(pltpu.make_async_copy(mid.at[part], dst.at[part], out_sem.at[n]))
            ins[n].start()
    for first, then in zip(ins, outs):
        first.wait()
        then.start()
    for cp in outs:
        cp.wait()


def local(tokens, up_weight, down_weight, grad_out):
    vm = pltpu.VMEM
    any_ = pl.BlockSpec(memory_space=pl.ANY)
    done = pl.pallas_call(
        kernel,
        name="ffn",
        out_shape=(
            jax.ShapeDtypeStruct((TOK, HALF), BF),
            jax.ShapeDtypeStruct((TOK, HALF), BF),
            jax.ShapeDtypeStruct((HALF, WIDE), BF),
            jax.ShapeDtypeStruct((WIDE, HALF), BF),
        ),
        in_specs=[any_] * 4,
        out_specs=(any_,) * 4,
        scratch_shapes=[
            vm((WIDE, WIDE), BF), vm((WIDE, WIDE), BF),
            vm((WIDE, WIDE), BF), vm((WIDE, WIDE), BF),
            vm((2, ROWS, HALF), BF), vm((2, ROWS, HALF), BF),
            vm((2, 2 * ROWS, HALF), BF), vm((2, 2 * ROWS, HALF), BF),
            vm((ROWS, HALF), BF), vm((ROWS, HALF), BF),
            vm((2, 2, ROWS, HALF), F32),
            vm((4 * TOK, HALF), F32),
            vm((4 * TOK, HALF), BF), vm((4 * TOK, HALF), BF),
            vm((8 * TOK, HALF), BF), vm((8 * TOK, HALF), BF),
            vm((12 * 128, HALF), BF), vm((12 * 128, HALF), BF),
            vm((28 * TOK, HALF), BF), vm((28 * TOK, HALF), BF),
            vm((8 * TOK, HALF), BF),
            vm((4 * TOK, HALF), BF), vm((4 * TOK, HALF), BF),
            vm((4 * TOK, HALF), F32), vm((2 * TOK, HALF), F32),
            vm((HALF, WIDE), BF), vm((WIDE, HALF), BF),
            vm((2 * TOK, HALF), BF),
            pltpu.SemaphoreType.DMA((192,)),
            pltpu.SemaphoreType.DMA((192,)),
            pltpu.SemaphoreType.DMA((16,)),
        ],
        compiler_params=pltpu.CompilerParams(
            collective_id=0, has_side_effects=True, vmem_limit_bytes=60 * 2**20
        ),
        cost_estimate=pl.CostEstimate(flops=12_600_000_000, bytes_accessed=10_000_000, transcendentals=300_000),
    )(tokens, up_weight, down_weight, grad_out)
    return pl.pallas_call(
        hand_on,
        name="hand_on",
        out_shape=[jax.ShapeDtypeStruct(x.shape, x.dtype) for x in done],
        in_specs=[any_] * 4,
        out_specs=[any_] * 4,
        scratch_shapes=[pltpu.VMEM(x.shape, x.dtype) for x in done]
        + [pltpu.SemaphoreType.DMA((2 * CUTS + 2,))] * 2,
        cost_estimate=pl.CostEstimate(flops=0, bytes_accessed=8_000_000, transcendentals=0),
    )(*done)


def solution(mesh):
    placed = (P("col", "row"), P("row", "col"), P("col", "row"), P("col", "row"))
    return jax.shard_map(
        local,
        mesh=mesh,
        in_specs=placed,
        out_specs=(P("col", "row"), P("col", "row"), P("row", "col"), P("col", "row")),
        check_vma=False,
    )
```

```python
import jax
import jax.numpy as jnp
from jax import lax
from jax.experimental import pallas as pl
from jax.experimental.pallas import tpu as pltpu
from jax.sharding import PartitionSpec as P

MESH = pl.DeviceIdType.MESH
BF = jnp.bfloat16
F32 = jnp.float32

TOK = 80
HALF = 640
WIDE = 1280
ROWS = 8 * TOK

PLACE = {0: 0, 1: 1, -1: 2, 2: 3, -2: 4, 3: 5, -3: 6, 4: 7}
SPAN = ((0, 1), (1, 2), (3, 2), (5, 2), (7, 1))
SUB = ((0, 48), (48, 32))

C0 = 0.7978845608028654
C1 = 0.044715

ORDER = (
    "W2s", "Gs", "W1s", "D", "Tzm2", "Tzp2", "Tzp3", "Tzm3", "P0", "Gzm2", "Gzp2", "Q1",
    "Tzp4", "Tzm4", "P1", "Gzm3", "Qx2", "Gzp3", "P2", "Py0ma", "Tzm5", "Py0pa", "Py0mb", "Tzp5",
    "Qx1", "Q0", "Tzm6", "Tzp6", "Qx0", "Gzp4", "Py0pb", "Q2", "Py0mc", "Qx3", "Gzm4", "Py0pc",
    "Qx4", "Gzm5", "Gzp5", "P3", "P4", "Py1ma", "Py1pa", "Px01", "Gzm6", "Py1mb", "Gzp6", "Px00",
    "Qy0ma", "Qy0pa", "Py1pb", "Q3", "Qx5", "Py1mc", "Qx6", "Py1pc", "Pe01", "Q4", "Qx7", "Qy0mb",
    "Pe00", "Qy0pb", "Qy0pc", "Px10", "Px11", "Pf0m", "U", "Qy1ma", "Qy1pa", "Qy1mb", "Qy1pb", "Pe10",
    "Tm", "Qy1mc", "Qy1pc", "Pf0p", "Pe11", "Pf1p", "Qy0mc", "Qe1", "Pf1m", "M1", "Gm", "Mu2",
    "Mu1", "M0", "Mw", "Qn1", "Qe0", "M4", "Mrp0", "Mu7", "M3", "Mrm1", "Qf1p", "Qf1m",
    "Mu5", "Mu6", "M2", "Qn0", "Am", "Mrp2", "Mu4", "Qf0p", "Mu3", "Mrm0", "Mrp1", "Mrm3",
    "I4", "Irp0", "Iu7", "I3", "Qf0m", "Mrm2", "Mrp4", "Iu5", "Iu6", "Irm1", "Mu0", "Mrp3",
    "Irm0", "DG3", "Irp2", "Mrm5", "Mrm4", "Irp1", "I2", "Iu3", "Mrp5", "I0", "Irm2", "Iu4",
    "Irp4", "Irm3", "I1", "Hm", "Irp3", "Iu1", "Mrm6", "Iu2", "Mrp6", "Irm4", "Iu0", "DG0",
    "Irp6", "Irm5", "DG1", "Irp5", "Iw", "DG2", "Irm6", "UG0", "Mt1", "Mt0", "It0", "It1",
    "UG1", "Mo", "Io",
)


def gelu(v):
    return 0.5 * v * (1.0 + jnp.tanh(C0 * (v + C1 * v * v * v)))


def gelu_slope(v):
    t = jnp.tanh(C0 * (v + C1 * v * v * v))
    return 0.5 * (1.0 + t) + 0.5 * v * (1.0 - t * t) * (C0 * (1.0 + 3.0 * C1 * v * v))


def rows_of(place, many=1):
    if isinstance(place, int):
        return pl.ds(place * TOK, many * TOK)
    return pl.ds(pl.multiple_of(place * TOK, TOK), many * TOK)


def cols_of(half):
    if isinstance(half, int):
        return pl.ds(half * HALF, HALF)
    return pl.ds(pl.multiple_of(half * HALF, HALF), HALF)


def kernel(
    tok_in, up_in, down_in, grad_in,
    mixed_out, igrad_out, upg_out, downg_out,
    up, down, up_t, down_t, tok, grad, act, hgrad, tok_o, grad_o,
    part, hid, h_send, h_recv, x_send, x_recv, y_send, y_recv, z_send, z_recv, u_send, u_recv, s_recv, w_send, w_recv, f_send, f_recv,
    upg, downg, small,
    ssem, rsem, lsem,
):
    r, c = lax.axis_index("row"), lax.axis_index("col")
    y, xh, k = r // 4, (r // 2) % 2, r % 2
    xl, z = c // 8, c % 8

    def row_id(yy, hh, kk):
        return (yy * 2 + hh) * 2 + kk

    mate = (row_id(y, xh, 1 - k), c)
    yside = {"p": (row_id((y + 1) % 4, xh, k), c), "m": (row_id((y + 3) % 4, xh, k), c)}
    across = (row_id(y, 1 - xh, k), c)
    zside = {"p": (r, xl * 8 + (z + 1) % 8), "m": (r, xl * 8 + (z + 7) % 8)}
    other_c = (1 - xl) * 8 + z
    other = ((row_id(y, xh, 0), other_c), (row_id(y, xh, 1), other_c))
    zstep_of = {"p": (z + 1) % 8, "m": (z + 7) % 8}
    slant = {d: (r, (1 - xl) * 8 + zstep_of[d]) for d in "pm"}
    givers = [(row_id(y, xh, q), k * 8 + zstep_of[d]) for d in "pm" for q in (0, 1)]

    count = [0, 0]
    ends = []
    msg = {}

    def sem():
        count[0] += 1
        return count[0] - 1

    def remote(src, dst, dev):
        i = sem()
        return pltpu.make_async_remote_copy(
            src_ref=src, dst_ref=dst, send_sem=ssem.at[i], recv_sem=rsem.at[i],
            device_id=dev, device_id_type=MESH,
        )

    def send(name, src, dst, dev):
        cp = remote(src, dst, dev)
        cp.start()
        ends.append(cp.wait_send)
        msg[name] = cp.wait_recv

    def got(*names):
        for name in names:
            wait = msg[name]
            if wait is not None:
                wait()
                msg[name] = None

    def lcopy(src, dst):
        cp = pltpu.make_async_copy(src, dst, lsem.at[count[1]])
        count[1] += 1
        cp.start()
        return cp.wait

    def unless(cond, f):
        def g():
            pl.when(cond)(f)

        return g

    own_rows = pl.ds(pl.multiple_of(k * HALF, HALF), HALF)
    msg["up"] = lcopy(up_in, up.at[own_rows])
    msg["down"] = lcopy(down_in, down.at[:, cols_of(k)])

    barrier = pltpu.get_barrier_semaphore()
    for dev in (mate, *yside.values(), across, *zside.values(), *other, *slant.values(), *givers):
        pl.semaphore_signal(barrier, inc=1, device_id=dev, device_id_type=MESH)
    pl.semaphore_wait(barrier, 14)

    def spread(name, src, buf):
        def to(place, col, core, i):
            j = sem()
            cp = pltpu.make_async_remote_copy(
                src_ref=src, dst_ref=buf.at[k, rows_of(place)], send_sem=ssem.at[j], recv_sem=rsem.at[i + k],
                device_id=(core, col), device_id_type=MESH,
            )
            return cp

        def arrived(place, i, h):
            return pltpu.make_async_copy(src, buf.at[h, rows_of(place)], rsem.at[i + h]).wait

        target = row_id(y, xh, xl)
        for straight in (True, False):
            for d in "pm":
                place = PLACE[-1 if d == "p" else 1]
                if straight:
                    msg[name + d] = sem(), sem()
                i = msg[name + d][0]
                cp = to(place, (xl if straight else 1 - xl) * 8 + zstep_of[d], target, i)
                cp.start()
                ends.append(cp.wait_send)
                if not straight:
                    for h in (0, 1):
                        msg[f"{name}z{d}{h if d == 'p' else 1 - h}"] = arrived(place, i, h)
        i, _ = sem(), sem()
        far = to(0, other_c, target, i)
        near = to(0, c, row_id(y, xh, 1 - k), i)
        stay = pltpu.make_async_copy(src, buf.at[k, rows_of(0)], rsem.at[i + k])
        far.start()
        pl.when(k != xl)(near.start)
        pl.when(k == xl)(stay.start)
        ends.append(far.wait_send)
        ends.append(unless(k != xl, near.wait_send))
        for h in (0, 1):
            msg[f"{name}s{h}"] = arrived(0, i, h)

    spread("T", tok_in, tok)

    tasks = {}
    tasks["W1s"] = lambda: send("W1", up_in, up.at[own_rows], mate)
    tasks["W2s"] = lambda: send("W2", down_in, down.at[:, cols_of(k)], mate)
    tasks["Gs"] = lambda: spread("G", grad_in, grad)

    def gather(name, buf):
        def source(off, h):
            if off == 0:
                return f"{name}s{h}"
            if off == 4:
                return f"{name}zp6" if h == 0 else f"{name}zm6"
            d, first = ("p", 0) if off < 0 else ("m", 1)
            return f"{name}z{d}{2 * (abs(off) - 1) + (0 if h == first else 1)}"

        def step(d, i):
            n, first, sign = i // 2, 0 if d == "p" else 1, -1 if d == "p" else 1
            h = first if i % 2 == 0 else 1 - first
            off, to = sign * n, sign * (n + 1)
            got(source(off, h))
            send(f"{name}z{d}{i}", buf.at[h, rows_of(PLACE[off])],
                 buf.at[h, rows_of(PLACE[4 if to == -4 else to])], zside[d])

        for d in "pm":
            for i in range(2, 7):
                tasks[f"{name}z{d}{i}"] = lambda d=d, i=i: step(d, i)
        return source

    tok_source, grad_source = gather("T", tok), gather("G", grad)

    def product(lhs, rhs, out, i):
        first, many = SPAN[i]
        rows = rows_of(first, many)
        v = (
            jnp.dot(lhs[0, rows, :], rhs[pl.ds(0, HALF), :], preferred_element_type=F32)
            + jnp.dot(lhs[1, rows, :], rhs[pl.ds(HALF, HALF), :], preferred_element_type=F32))
        out[0, rows, :] = v[:, :HALF]
        out[1, rows, :] = v[:, HALF:]

    def turn(src, dst):
        def body(n, _):
            cols = pl.ds(pl.multiple_of(n * 256, 256), 256)
            dst[:, cols] = src[cols, :].T
            return 0

        lax.fori_loop(0, WIDE // 256, body, 0)

    def turn_up():
        got("up", "W1")
        turn(up, up_t)

    def turn_down():
        got("down", "W2")
        turn(down, down_t)

    tasks["U"], tasks["D"] = turn_up, turn_down

    def offs(i):
        return (i,) if i in (0, 4) else (i, -i)

    def way(n, R, source, lhs, rhs, N, lhs2, rhs2, finish):
        src = part.at[n]

        def first(i):
            got("up", "W1", *(source(o, h) for o in offs(i) for h in (0, 1)))
            product(lhs, rhs, src, i)

        for i in range(5):
            tasks[f"{R}{i}"] = lambda i=i: first(i)

        def fbuf(b, d, s):
            return rows_of(b * 6 + "pm".index(d) * 3 + "abc".index(s))

        def ywhole(b, d, s):
            near = 1 if d == "p" else 3
            h = 0 if d == "p" else 1
            if s == "b":
                h = 1 - h
            v = src[h, rows_of(b * 4 + (y + (2 if s == "a" else near)) % 4), :]
            if s == "c":
                got(f"{R}y{b}{d}a")
                v = v + y_recv[fbuf(b, d, "a"), :].astype(F32)
            mine = fbuf(b, d, s)
            y_send[mine, :] = v.astype(BF)
            send(f"{R}y{b}{d}{s}", y_send.at[mine], y_recv.at[mine], yside[d])

        def xwhole(b, h):
            p, m = ("c", "b") if h == 0 else ("b", "c")
            got(f"{R}y{b}p{p}", f"{R}y{b}m{m}")
            rows = rows_of(b * 2 + h)
            t = (src[h, rows_of(b * 4 + y), :] + y_recv[fbuf(b, "p", p), :].astype(F32)
                 + y_recv[fbuf(b, "m", m), :].astype(F32))
            hid[rows, :] = t
            h_send[rows, :] = t.astype(BF)
            send(f"{R}x{b}{h}", h_send.at[rows], h_recv.at[rows], across)

        def ewhole(b, h):
            got(f"{R}x{b}{h}")
            rows = rows_of(b * 2 + h)
            mine = lhs2.at[h, rows_of(b * 4 + y)]
            mine[...] = finish(hid[rows, :] + h_recv[rows, :].astype(F32), rows).astype(BF)
            for d in "pm":
                send(f"{R}o{b}{h}{d}", mine, mine, yside[d])

        def fwhole(b, d):
            h, yy = (0, (y + 3) % 4) if d == "p" else (1, (y + 1) % 4)
            got(f"{R}o{b}{h}{d}")
            p = lhs2.at[h, rows_of(b * 4 + yy)]
            send(f"{R}f{b}{d}", p, p, yside[d])

        for b in (0, 1) if n == 0 else ():
            for d in "pm":
                for s in "abc":
                    tasks[f"{R}y{b}{d}{s}"] = lambda b=b, d=d, s=s: ywhole(b, d, s)
                tasks[f"{R}f{b}{d}"] = lambda b=b, d=d: fwhole(b, d)
            for h in (0, 1):
                tasks[f"{R}x{b}{h}"] = lambda b=b, h=h: xwhole(b, h)
                tasks[f"{R}e{b}{h}"] = lambda b=b, h=h: ewhole(b, h)

        def xbuf(p):
            return rows_of(p)

        def xstep(p):
            x_send[xbuf(p), :] = src[1 - xh, rows_of(p), :].astype(BF)
            send(f"{R}x{p}", x_send.at[xbuf(p)], x_recv.at[xbuf(p)], across)

        def paired(p, r):
            start, many = SUB[r]
            rows = pl.ds(pl.multiple_of(p * TOK + start, 16), many)
            far = pl.ds(pl.multiple_of(p * TOK + start, 16), many)
            return src[xh, rows, :] + x_recv[far, :].astype(F32)

        def ybuf(b, d, s, r):
            return pl.ds(12 * TOK + (b * 6 + "pm".index(d) * 3 + "abc".index(s)) * SUB[0][1], SUB[r][1])

        def ystep(b, d, s):
            got(*(f"{R}x{b * 4 + i}" for i in range(4)))
            near = 1 if d == "p" else 3
            r = b if d == "p" else 1 - b
            if s == "b":
                r = 1 - r
            v = paired(b * 4 + (y + (2 if s == "a" else near)) % 4, r)
            if s == "c":
                got(f"{R}y{b}{d}a")
                v = v + y_recv[ybuf(b, d, "a", r), :].astype(F32)
            mine = ybuf(b, d, s, r)
            y_send[mine, :] = v.astype(BF)
            send(f"{R}y{b}{d}{s}", y_send.at[mine], y_recv.at[mine], yside[d])

        def piece(b, yy, h):
            return lhs2.at[h, rows_of(b * 4 + yy)]

        def estep(b):
            got(*(f"{R}y{b}{d}{s}" for d in "pm" for s in "bc"))
            for r in (0, 1):
                p, m = ("c", "b") if r == b else ("b", "c")
                v = (paired(b * 4 + y, r) + y_recv[ybuf(b, "p", p, r), :].astype(F32)
                     + y_recv[ybuf(b, "m", m, r), :].astype(F32))
                start, many = SUB[r]
                v = finish(v, pl.ds(pl.multiple_of((b * 2 + xh) * TOK + start, 16), many)).astype(BF)
                lhs2[xh, pl.ds(pl.multiple_of((b * 4 + y) * TOK + start, 16), many), :] = v
            mine = piece(b, y, xh)
            for d in "pm":
                send(f"{R}o{b}{d}", mine, mine, yside[d])
            send(f"{R}a{b}", mine, mine, across)

        def nstep(b):
            got(f"{R}a{b}")
            theirs = piece(b, y, 1 - xh)
            for d in "pm":
                send(f"{R}n{b}{d}", theirs, theirs, yside[d])

        def fstep(b, d):
            if d == "p":
                got(f"{R}o{b}p")
                p = piece(b, (y + 3) % 4, xh)
            else:
                got(f"{R}n{b}m")
                p = piece(b, (y + 1) % 4, 1 - xh)
            send(f"{R}f{b}{d}", p, p, yside[d])

        for p in range(8 if n == 1 else 0):
            tasks[f"{R}x{p}"] = lambda p=p: xstep(p)
        for b in (0, 1) if n == 1 else ():
            for d in "pm":
                for s in "abc":
                    tasks[f"{R}y{b}{d}{s}"] = lambda b=b, d=d, s=s: ystep(b, d, s)
                tasks[f"{R}f{b}{d}"] = lambda b=b, d=d: fstep(b, d)
            tasks[f"{R}e{b}"] = lambda b=b: estep(b)
            tasks[f"{R}n{b}"] = lambda b=b: nstep(b)

        def second(i):
            for b in {0: (0,), 1: (0,), 2: (0, 1), 3: (1,), 4: (1,)}[i]:
                got(*(f"{R}{q}{b}{d}" for q in "fon" for d in "pm" if f"{R}{q}{b}{d}" in msg),
                    *(f"{R}o{b}{h}{d}" for h in (0, 1) for d in "pm" if f"{R}o{b}{h}{d}" in msg))
            got("down", "W2")
            product(lhs2, rhs2, src, i)

        for i in range(5):
            tasks[f"{N}{i}"] = lambda i=i: second(i)

        def zbuf(d, i):
            return rows_of(n * 14 + "pm".index(d) * 7 + i)

        def ubuf(p):
            return rows_of(n * 8 + p)

        def ustep(p):
            cp = remote(u_send.at[ubuf(p)], u_recv.at[ubuf(p)], (r, other_c))

            @pl.when(xl != k)
            def _():
                u_send[ubuf(p), :] = src[1, rows_of(p), :].astype(BF)
                cp.start()

            ends.append(unless(xl != k, cp.wait_send))
            msg[f"{N}u{p}"] = cp.wait_recv

        for p in range(8):
            tasks[f"{N}u{p}"] = lambda p=p: ustep(p)

        def zstep(d, i):
            first = 0 if d == "p" else 1
            h = first if i % 2 == 0 else 1 - first
            o = 4 - (i + 1) // 2
            place = PLACE[o if d == "p" or o == 4 else -o]
            mine = zbuf(d, i)
            straight = remote(z_send.at[mine], z_recv.at[mine], zside[d])
            msg[f"{N}r{d}{i}"] = straight.wait_recv
            if h == 1:
                @pl.when(xl == k)
                def _():
                    msg[f"{N}u{place}"]()
                    v = src[1, rows_of(place), :] + u_recv[ubuf(place), :].astype(F32)
                    if i >= 2:
                        msg[f"{N}r{d}{i - 2}"]()
                        v = v + z_recv[zbuf(d, i - 2), :].astype(F32)
                    z_send[mine, :] = v.astype(BF)
                    straight.start()

                ends.append(unless(xl == k, straight.wait_send))
                return
            v = src[0, rows_of(place), :]
            if i >= 2:
                msg[f"{N}r{d}{i - 2}"]()
                v = v + z_recv[zbuf(d, i - 2), :].astype(F32)
            z_send[mine, :] = v.astype(BF)
            if i < 5:
                straight.start()
                ends.append(straight.wait_send)
                return
            there = rows_of(n * 2 + "pm".index(d))
            aslant = remote(z_send.at[mine], s_recv.at[there], slant[d])
            pl.when(xl == k)(straight.start)
            pl.when(xl != k)(aslant.start)
            ends.append(unless(xl == k, straight.wait_send))
            ends.append(unless(xl != k, aslant.wait_send))
            msg[f"{N}s{d}"] = aslant.wait_recv

        for d in "pm":
            for i in range(7):
                tasks[f"{N}r{d}{i}"] = lambda d=d, i=i: zstep(d, i)

        def wstep():
            mine = rows_of(n)
            cp = remote(w_send.at[mine], w_recv.at[mine], (r, other_c))

            @pl.when(xl != k)
            def _():
                w_send[mine, :] = src[0, rows_of(0), :].astype(BF)
                cp.start()

            ends.append(unless(xl != k, cp.wait_send))
            msg[f"{N}w"] = cp.wait_recv

        def tstep(h):
            mine = rows_of(n * 2 + h)
            cp = remote(f_send.at[mine], f_recv.at[rows_of(n)], mate)

            @pl.when(xl == k)
            def _():
                v = src[h, rows_of(0), :]
                if h == 0:
                    msg[f"{N}w"]()
                    v = v + w_recv[rows_of(n), :].astype(F32)
                else:
                    msg[f"{N}u0"]()
                    v = v + u_recv[ubuf(0), :].astype(F32)
                for d in "pm":
                    i = 6 if (h == 0) == (d == "p") else 5
                    msg[f"{N}r{d}{i}"]()
                    v = v + z_recv[zbuf(d, i), :].astype(F32)
                    if h == 0:
                        msg[f"{N}s{d}"]()
                        v = v + s_recv[rows_of(n * 2 + "pm".index(d)), :].astype(F32)
                f_send[mine, :] = v
                pl.when(k != h)(cp.start)

            give = jnp.logical_and(xl == k, k != h)
            ends.append(unless(give, cp.wait_send))
            msg[f"{N}t{h}"] = unless(jnp.logical_and(xl != k, k == h), cp.wait_recv)

        def ostep():
            mine = rows_of(n)
            msg[f"{N}t0"]()
            msg[f"{N}t1"]()

            @pl.when(xl != k)
            def _():
                small[mine, :] = f_recv[mine, :].astype(BF)

            @pl.when(xl == k)
            def _():
                small[mine, :] = f_send[rows_of(n * 2 + k), :].astype(BF)

            ends.append(lcopy(small.at[mine], (mixed_out, igrad_out)[n]))

        tasks[f"{N}w"] = wstep
        tasks[f"{N}t0"], tasks[f"{N}t1"], tasks[f"{N}o"] = lambda: tstep(0), lambda: tstep(1), ostep

    def forward(v, rows):
        hid[rows, :] = v
        return gelu(v)

    def backward(v, rows):
        return v * gelu_slope(hid[rows, :])

    way(0, "P", tok_source, tok, up, "M", act, down, forward)
    way(1, "Q", grad_source, grad, down_t, "I", hgrad, up_t, backward)

    low, high = pl.ds(0, ROWS), pl.ds(ROWS, ROWS)

    def swap(name, source, buf, out):
        got(*(source(o, h) for o in PLACE for h in (0, 1)))
        send(name, buf.at[1 - k], out, mate)

    tasks["Tm"] = lambda: swap("Tm", tok_source, tok, tok_o)
    tasks["Gm"] = lambda: swap("Gm", grad_source, grad, grad_o)

    def twin(name, buf):
        for h in (0, 1):
            send(f"{name}{h}", buf.at[h, low], buf.at[h, high], mate)

    tasks["Am"] = lambda: twin("Am", act)
    tasks["Hm"] = lambda: twin("Hm", hgrad)

    def outer(a, b):
        return lax.dot_general(a, b, (((0,), (0,)), ((), ())), preferred_element_type=F32)

    def dg(i):
        got("Gm", "Am0", "Am1")
        for h, first, many in (((0, 0, 256),), ((0, 256, 384),), ((1, 0, 256),), ((1, 256, 384),))[i]:
            cols, rows = pl.ds(first, many), pl.ds(h * HALF + first, many)
            v = outer(act[h, low, cols], grad[k]) + outer(act[h, high, cols], grad_o[...])
            downg[rows, :] = v.astype(BF)
            ends.append(lcopy(downg.at[rows], downg_out.at[rows]))

    def ug(i):
        got("Tm", "Hm0", "Hm1")
        rows = pl.ds(*((0, 256), (256, 384))[i])
        for h in (0, 1):
            v = outer(tok[k, :, rows], hgrad[h, low, :]) + outer(tok_o[:, rows], hgrad[h, high, :])
            upg[rows, cols_of(h)] = v.astype(BF)
        ends.append(lcopy(upg.at[rows], upg_out.at[rows]))

    for i in range(4):
        tasks[f"DG{i}"] = lambda i=i: dg(i)
    for i in range(2):
        tasks[f"UG{i}"] = lambda i=i: ug(i)

    for name in ORDER[:-1]:
        tasks[name]()
    for end in ends:
        end()
    ends.clear()
    tasks[ORDER[-1]]()
    for end in ends:
        end()


CUTS = 4


def hand_on(a, b, c, d, a_out, b_out, c_out, d_out, a_mid, b_mid, c_mid, d_mid, in_sem, out_sem):
    ins, outs = [], []
    for src, mid, dst, many in ((c, c_mid, c_out, CUTS), (d, d_mid, d_out, CUTS), (a, a_mid, a_out, 1), (b, b_mid, b_out, 1)):
        rows = src.shape[0] // many
        for i in range(many):
            part = pl.ds(i * rows, rows)
            n = len(ins)
            ins.append(pltpu.make_async_copy(src.at[part], mid.at[part], in_sem.at[n]))
            outs.append(pltpu.make_async_copy(mid.at[part], dst.at[part], out_sem.at[n]))
            ins[n].start()
    for first, then in zip(ins, outs):
        first.wait()
        then.start()
    for cp in outs:
        cp.wait()


def local(tokens, up_weight, down_weight, grad_out):
    vm = pltpu.VMEM
    any_ = pl.BlockSpec(memory_space=pl.ANY)
    done = pl.pallas_call(
        kernel,
        name="ffn",
        out_shape=(
            jax.ShapeDtypeStruct((TOK, HALF), BF),
            jax.ShapeDtypeStruct((TOK, HALF), BF),
            jax.ShapeDtypeStruct((HALF, WIDE), BF),
            jax.ShapeDtypeStruct((WIDE, HALF), BF),
        ),
        in_specs=[any_] * 4,
        out_specs=(any_,) * 4,
        scratch_shapes=[
            vm((WIDE, WIDE), BF), vm((WIDE, WIDE), BF),
            vm((WIDE, WIDE), BF), vm((WIDE, WIDE), BF),
            vm((2, ROWS, HALF), BF), vm((2, ROWS, HALF), BF),
            vm((2, 2 * ROWS, HALF), BF), vm((2, 2 * ROWS, HALF), BF),
            vm((ROWS, HALF), BF), vm((ROWS, HALF), BF),
            vm((2, 2, ROWS, HALF), F32),
            vm((4 * TOK, HALF), F32),
            vm((4 * TOK, HALF), BF), vm((4 * TOK, HALF), BF),
            vm((8 * TOK, HALF), BF), vm((8 * TOK, HALF), BF),
            vm((12 * 128, HALF), BF), vm((12 * 128, HALF), BF),
            vm((28 * TOK, HALF), BF), vm((28 * TOK, HALF), BF),
            vm((16 * TOK, HALF), BF), vm((16 * TOK, HALF), BF),
            vm((4 * TOK, HALF), BF),
            vm((2 * TOK, HALF), BF), vm((2 * TOK, HALF), BF),
            vm((4 * TOK, HALF), F32), vm((2 * TOK, HALF), F32),
            vm((HALF, WIDE), BF), vm((WIDE, HALF), BF),
            vm((2 * TOK, HALF), BF),
            pltpu.SemaphoreType.DMA((192,)),
            pltpu.SemaphoreType.DMA((192,)),
            pltpu.SemaphoreType.DMA((16,)),
        ],
        compiler_params=pltpu.CompilerParams(
            collective_id=0, has_side_effects=True, vmem_limit_bytes=60 * 2**20
        ),
        cost_estimate=pl.CostEstimate(flops=12_600_000_000, bytes_accessed=10_000_000, transcendentals=300_000),
    )(tokens, up_weight, down_weight, grad_out)
    return pl.pallas_call(
        hand_on,
        name="hand_on",
        out_shape=[jax.ShapeDtypeStruct(x.shape, x.dtype) for x in done],
        in_specs=[any_] * 4,
        out_specs=[any_] * 4,
        scratch_shapes=[pltpu.VMEM(x.shape, x.dtype) for x in done]
        + [pltpu.SemaphoreType.DMA((2 * CUTS + 2,))] * 2,
        cost_estimate=pl.CostEstimate(flops=0, bytes_accessed=8_000_000, transcendentals=0),
    )(*done)


def solution(mesh):
    placed = (P("col", "row"), P("row", "col"), P("col", "row"), P("col", "row"))
    return jax.shard_map(
        local,
        mesh=mesh,
        in_specs=placed,
        out_specs=(P("col", "row"), P("col", "row"), P("row", "col"), P("col", "row")),
        check_vma=False,
    )
```

```python
import jax
import jax.numpy as jnp
from jax import lax
from jax.experimental import pallas as pl
from jax.experimental.pallas import tpu as pltpu
from jax.sharding import PartitionSpec as P

MESH = pl.DeviceIdType.MESH
BF = jnp.bfloat16
F32 = jnp.float32

TOK = 80
HALF = 640
WIDE = 1280
ROWS = 8 * TOK

PLACE = {0: 0, 1: 1, -1: 2, 2: 3, -2: 4, 3: 5, -3: 6, 4: 7}
SPAN = ((0, 1), (1, 2), (3, 2), (5, 2), (7, 1))
SUB = ((0, 48), (48, 32))

C0 = 0.7978845608028654
C1 = 0.044715

ORDER = (
    "W2s", "Gs", "W1s", "D", "Tzm2", "Tzp2", "Tzp3", "Tzm3", "P0", "Gzm2", "Gzp2", "Q1",
    "Tzp4", "Tzm4", "P1", "Gzm3", "Qx2", "Gzp3", "P2", "Py0ma", "Tzm5", "Py0pa", "Py0mb", "Tzp5",
    "Qx1", "Q0", "Tzm6", "Tzp6", "Qx0", "Gzp4", "Py0pb", "Q2", "Py0mc", "Qx3", "Gzm4", "Py0pc",
    "Qx4", "Gzm5", "Gzp5", "P3", "P4", "Py1ma", "Py1pa", "Px01", "Gzm6", "Py1mb", "Gzp6", "Px00",
    "Qy0ma", "Qy0pa", "Py1pb", "Q3", "Qx5", "Py1mc", "Qx6", "Py1pc", "Pe01", "Q4", "Qx7", "Qy0mb",
    "Pe00", "Qy0pb", "Qy0pc", "Px10", "Px11", "Pf0m", "U", "Qy1ma", "Qy1pa", "Qy1mb", "Qy1pb", "Pe10",
    "Tm", "Qy1mc", "Qy1pc", "Pf0p", "Pe11", "Pf1p", "Qy0mc", "Qe1", "Pf1m", "M1", "Gm", "Mu2",
    "Mu1", "M0", "Mw", "Qn1", "Qe0", "M4", "Mrp0", "Mu7", "M3", "Mrm1", "Qf1p", "Qf1m",
    "Mu5", "Mu6", "M2", "Qn0", "Am", "Mrp2", "Mu4", "Qf0p", "Mu3", "Mrm0", "Mrp1", "Mrm3",
    "I4", "Irp0", "Iu7", "I3", "Qf0m", "Mrm2", "Mrp4", "Iu5", "Iu6", "Irm1", "Mu0", "Mrp3",
    "Irm0", "DG3", "Irp2", "Mrm5", "Mrm4", "Irp1", "I2", "Iu3", "Mrp5", "I0", "Irm2", "Iu4",
    "Irp4", "Irm3", "I1", "Hm", "Irp3", "Iu1", "Mrm6", "Iu2", "Mrp6", "Irm4", "Iu0", "DG0",
    "Irp6", "Irm5", "DG1", "Irp5", "Iw", "DG2", "Irm6", "UG0", "Mt1", "Mt0", "It0", "It1",
    "UG1", "Mo", "Io",
)


def gelu(v):
    return 0.5 * v * (1.0 + jnp.tanh(C0 * (v + C1 * v * v * v)))


def gelu_slope(v):
    t = jnp.tanh(C0 * (v + C1 * v * v * v))
    return 0.5 * (1.0 + t) + 0.5 * v * (1.0 - t * t) * (C0 * (1.0 + 3.0 * C1 * v * v))


def rows_of(place, many=1):
    if isinstance(place, int):
        return pl.ds(place * TOK, many * TOK)
    return pl.ds(pl.multiple_of(place * TOK, TOK), many * TOK)


def cols_of(half):
    if isinstance(half, int):
        return pl.ds(half * HALF, HALF)
    return pl.ds(pl.multiple_of(half * HALF, HALF), HALF)


def kernel(
    tok_in, up_in, down_in, grad_in,
    mixed_out, igrad_out, upg_out, downg_out,
    up, down, up_t, down_t, tok, grad, act, hgrad, tok_o, grad_o,
    part, hid, h_send, h_recv, x_send, x_recv, y_send, y_recv, z_send, z_recv, u_send, u_recv, s_recv, w_send, w_recv,
    upg, downg, small,
    ssem, rsem, lsem,
):
    r, c = lax.axis_index("row"), lax.axis_index("col")
    y, xh, k = r // 4, (r // 2) % 2, r % 2
    xl, z = c // 8, c % 8

    def row_id(yy, hh, kk):
        return (yy * 2 + hh) * 2 + kk

    mate = (row_id(y, xh, 1 - k), c)
    yside = {"p": (row_id((y + 1) % 4, xh, k), c), "m": (row_id((y + 3) % 4, xh, k), c)}
    across = (row_id(y, 1 - xh, k), c)
    zside = {"p": (r, xl * 8 + (z + 1) % 8), "m": (r, xl * 8 + (z + 7) % 8)}
    other_c = (1 - xl) * 8 + z
    other = ((row_id(y, xh, 0), other_c), (row_id(y, xh, 1), other_c))
    zstep_of = {"p": (z + 1) % 8, "m": (z + 7) % 8}
    slant = {d: (r, (1 - xl) * 8 + zstep_of[d]) for d in "pm"}
    givers = [(row_id(y, xh, q), k * 8 + zstep_of[d]) for d in "pm" for q in (0, 1)]

    count = [0, 0]
    ends = []
    msg = {}

    def sem():
        count[0] += 1
        return count[0] - 1

    def remote(src, dst, dev):
        i = sem()
        return pltpu.make_async_remote_copy(
            src_ref=src, dst_ref=dst, send_sem=ssem.at[i], recv_sem=rsem.at[i],
            device_id=dev, device_id_type=MESH,
        )

    def send(name, src, dst, dev):
        cp = remote(src, dst, dev)
        cp.start()
        ends.append(cp.wait_send)
        msg[name] = cp.wait_recv

    def got(*names):
        for name in names:
            wait = msg[name]
            if wait is not None:
                wait()
                msg[name] = None

    def lcopy(src, dst):
        cp = pltpu.make_async_copy(src, dst, lsem.at[count[1]])
        count[1] += 1
        cp.start()
        return cp.wait

    def unless(cond, f):
        def g():
            pl.when(cond)(f)

        return g

    own_rows = pl.ds(pl.multiple_of(k * HALF, HALF), HALF)
    msg["up"] = lcopy(up_in, up.at[own_rows])
    msg["down"] = lcopy(down_in, down.at[:, cols_of(k)])

    barrier = pltpu.get_barrier_semaphore()
    for dev in (mate, *yside.values(), across, *zside.values(), *other, *slant.values(), *givers):
        pl.semaphore_signal(barrier, inc=1, device_id=dev, device_id_type=MESH)
    pl.semaphore_wait(barrier, 14)

    def spread(name, src, buf):
        def to(place, col, core, i):
            j = sem()
            cp = pltpu.make_async_remote_copy(
                src_ref=src, dst_ref=buf.at[k, rows_of(place)], send_sem=ssem.at[j], recv_sem=rsem.at[i + k],
                device_id=(core, col), device_id_type=MESH,
            )
            return cp

        def arrived(place, i, h):
            return pltpu.make_async_copy(src, buf.at[h, rows_of(place)], rsem.at[i + h]).wait

        target = row_id(y, xh, xl)
        for straight in (True, False):
            for d in "pm":
                place = PLACE[-1 if d == "p" else 1]
                if straight:
                    msg[name + d] = sem(), sem()
                i = msg[name + d][0]
                cp = to(place, (xl if straight else 1 - xl) * 8 + zstep_of[d], target, i)
                cp.start()
                ends.append(cp.wait_send)
                if not straight:
                    for h in (0, 1):
                        msg[f"{name}z{d}{h if d == 'p' else 1 - h}"] = arrived(place, i, h)
        i, _ = sem(), sem()
        far = to(0, other_c, target, i)
        near = to(0, c, row_id(y, xh, 1 - k), i)
        stay = pltpu.make_async_copy(src, buf.at[k, rows_of(0)], rsem.at[i + k])
        far.start()
        pl.when(k != xl)(near.start)
        pl.when(k == xl)(stay.start)
        ends.append(far.wait_send)
        ends.append(unless(k != xl, near.wait_send))
        for h in (0, 1):
            msg[f"{name}s{h}"] = arrived(0, i, h)

    spread("T", tok_in, tok)

    tasks = {}
    tasks["W1s"] = lambda: send("W1", up_in, up.at[own_rows], mate)
    tasks["W2s"] = lambda: send("W2", down_in, down.at[:, cols_of(k)], mate)
    tasks["Gs"] = lambda: spread("G", grad_in, grad)

    def gather(name, buf):
        def source(off, h):
            if off == 0:
                return f"{name}s{h}"
            if off == 4:
                return f"{name}zp6" if h == 0 else f"{name}zm6"
            d, first = ("p", 0) if off < 0 else ("m", 1)
            return f"{name}z{d}{2 * (abs(off) - 1) + (0 if h == first else 1)}"

        def step(d, i):
            n, first, sign = i // 2, 0 if d == "p" else 1, -1 if d == "p" else 1
            h = first if i % 2 == 0 else 1 - first
            off, to = sign * n, sign * (n + 1)
            got(source(off, h))
            send(f"{name}z{d}{i}", buf.at[h, rows_of(PLACE[off])],
                 buf.at[h, rows_of(PLACE[4 if to == -4 else to])], zside[d])

        for d in "pm":
            for i in range(2, 7):
                tasks[f"{name}z{d}{i}"] = lambda d=d, i=i: step(d, i)
        return source

    tok_source, grad_source = gather("T", tok), gather("G", grad)

    def product(lhs, rhs, out, i):
        first, many = SPAN[i]
        rows = rows_of(first, many)
        v = (
            jnp.dot(lhs[0, rows, :], rhs[pl.ds(0, HALF), :], preferred_element_type=F32)
            + jnp.dot(lhs[1, rows, :], rhs[pl.ds(HALF, HALF), :], preferred_element_type=F32))
        out[0, rows, :] = v[:, :HALF]
        out[1, rows, :] = v[:, HALF:]

    def turn(src, dst):
        def body(n, _):
            cols = pl.ds(pl.multiple_of(n * 256, 256), 256)
            dst[:, cols] = src[cols, :].T
            return 0

        lax.fori_loop(0, WIDE // 256, body, 0)

    def turn_up():
        got("up", "W1")
        turn(up, up_t)

    def turn_down():
        got("down", "W2")
        turn(down, down_t)

    tasks["U"], tasks["D"] = turn_up, turn_down

    def offs(i):
        return (i,) if i in (0, 4) else (i, -i)

    def way(n, R, source, lhs, rhs, N, lhs2, rhs2, finish):
        src = part.at[n]

        def first(i):
            got("up", "W1", *(source(o, h) for o in offs(i) for h in (0, 1)))
            product(lhs, rhs, src, i)

        for i in range(5):
            tasks[f"{R}{i}"] = lambda i=i: first(i)

        def fbuf(b, d, s):
            return rows_of(b * 6 + "pm".index(d) * 3 + "abc".index(s))

        def ywhole(b, d, s):
            near = 1 if d == "p" else 3
            h = 0 if d == "p" else 1
            if s == "b":
                h = 1 - h
            v = src[h, rows_of(b * 4 + (y + (2 if s == "a" else near)) % 4), :]
            if s == "c":
                got(f"{R}y{b}{d}a")
                v = v + y_recv[fbuf(b, d, "a"), :].astype(F32)
            mine = fbuf(b, d, s)
            y_send[mine, :] = v.astype(BF)
            send(f"{R}y{b}{d}{s}", y_send.at[mine], y_recv.at[mine], yside[d])

        def xwhole(b, h):
            p, m = ("c", "b") if h == 0 else ("b", "c")
            got(f"{R}y{b}p{p}", f"{R}y{b}m{m}")
            rows = rows_of(b * 2 + h)
            t = (src[h, rows_of(b * 4 + y), :] + y_recv[fbuf(b, "p", p), :].astype(F32)
                 + y_recv[fbuf(b, "m", m), :].astype(F32))
            hid[rows, :] = t
            h_send[rows, :] = t.astype(BF)
            send(f"{R}x{b}{h}", h_send.at[rows], h_recv.at[rows], across)

        def ewhole(b, h):
            got(f"{R}x{b}{h}")
            rows = rows_of(b * 2 + h)
            mine = lhs2.at[h, rows_of(b * 4 + y)]
            mine[...] = finish(hid[rows, :] + h_recv[rows, :].astype(F32), rows).astype(BF)
            for d in "pm":
                send(f"{R}o{b}{h}{d}", mine, mine, yside[d])

        def fwhole(b, d):
            h, yy = (0, (y + 3) % 4) if d == "p" else (1, (y + 1) % 4)
            got(f"{R}o{b}{h}{d}")
            p = lhs2.at[h, rows_of(b * 4 + yy)]
            send(f"{R}f{b}{d}", p, p, yside[d])

        for b in (0, 1) if n == 0 else ():
            for d in "pm":
                for s in "abc":
                    tasks[f"{R}y{b}{d}{s}"] = lambda b=b, d=d, s=s: ywhole(b, d, s)
                tasks[f"{R}f{b}{d}"] = lambda b=b, d=d: fwhole(b, d)
            for h in (0, 1):
                tasks[f"{R}x{b}{h}"] = lambda b=b, h=h: xwhole(b, h)
                tasks[f"{R}e{b}{h}"] = lambda b=b, h=h: ewhole(b, h)

        def xbuf(p):
            return rows_of(p)

        def xstep(p):
            x_send[xbuf(p), :] = src[1 - xh, rows_of(p), :].astype(BF)
            send(f"{R}x{p}", x_send.at[xbuf(p)], x_recv.at[xbuf(p)], across)

        def paired(p, r):
            start, many = SUB[r]
            rows = pl.ds(pl.multiple_of(p * TOK + start, 16), many)
            far = pl.ds(pl.multiple_of(p * TOK + start, 16), many)
            return src[xh, rows, :] + x_recv[far, :].astype(F32)

        def ybuf(b, d, s, r):
            return pl.ds(12 * TOK + (b * 6 + "pm".index(d) * 3 + "abc".index(s)) * SUB[0][1], SUB[r][1])

        def ystep(b, d, s):
            got(*(f"{R}x{b * 4 + i}" for i in range(4)))
            near = 1 if d == "p" else 3
            r = b if d == "p" else 1 - b
            if s == "b":
                r = 1 - r
            v = paired(b * 4 + (y + (2 if s == "a" else near)) % 4, r)
            if s == "c":
                got(f"{R}y{b}{d}a")
                v = v + y_recv[ybuf(b, d, "a", r), :].astype(F32)
            mine = ybuf(b, d, s, r)
            y_send[mine, :] = v.astype(BF)
            send(f"{R}y{b}{d}{s}", y_send.at[mine], y_recv.at[mine], yside[d])

        def piece(b, yy, h):
            return lhs2.at[h, rows_of(b * 4 + yy)]

        def estep(b):
            got(*(f"{R}y{b}{d}{s}" for d in "pm" for s in "bc"))
            for r in (0, 1):
                p, m = ("c", "b") if r == b else ("b", "c")
                v = (paired(b * 4 + y, r) + y_recv[ybuf(b, "p", p, r), :].astype(F32)
                     + y_recv[ybuf(b, "m", m, r), :].astype(F32))
                start, many = SUB[r]
                v = finish(v, pl.ds(pl.multiple_of((b * 2 + xh) * TOK + start, 16), many)).astype(BF)
                lhs2[xh, pl.ds(pl.multiple_of((b * 4 + y) * TOK + start, 16), many), :] = v
            mine = piece(b, y, xh)
            for d in "pm":
                send(f"{R}o{b}{d}", mine, mine, yside[d])
            send(f"{R}a{b}", mine, mine, across)

        def nstep(b):
            got(f"{R}a{b}")
            theirs = piece(b, y, 1 - xh)
            for d in "pm":
                send(f"{R}n{b}{d}", theirs, theirs, yside[d])

        def fstep(b, d):
            if d == "p":
                got(f"{R}o{b}p")
                p = piece(b, (y + 3) % 4, xh)
            else:
                got(f"{R}n{b}m")
                p = piece(b, (y + 1) % 4, 1 - xh)
            send(f"{R}f{b}{d}", p, p, yside[d])

        for p in range(8 if n == 1 else 0):
            tasks[f"{R}x{p}"] = lambda p=p: xstep(p)
        for b in (0, 1) if n == 1 else ():
            for d in "pm":
                for s in "abc":
                    tasks[f"{R}y{b}{d}{s}"] = lambda b=b, d=d, s=s: ystep(b, d, s)
                tasks[f"{R}f{b}{d}"] = lambda b=b, d=d: fstep(b, d)
            tasks[f"{R}e{b}"] = lambda b=b: estep(b)
            tasks[f"{R}n{b}"] = lambda b=b: nstep(b)

        def second(i):
            for b in {0: (0,), 1: (0,), 2: (0, 1), 3: (1,), 4: (1,)}[i]:
                got(*(f"{R}{q}{b}{d}" for q in "fon" for d in "pm" if f"{R}{q}{b}{d}" in msg),
                    *(f"{R}o{b}{h}{d}" for h in (0, 1) for d in "pm" if f"{R}o{b}{h}{d}" in msg))
            got("down", "W2")
            product(lhs2, rhs2, src, i)

        for i in range(5):
            tasks[f"{N}{i}"] = lambda i=i: second(i)

        def zbuf(d, i):
            return rows_of(n * 14 + "pm".index(d) * 7 + i)

        def ubuf(p):
            return rows_of(n * 8 + p)

        def ustep(p):
            cp = remote(u_send.at[ubuf(p)], u_recv.at[ubuf(p)], (r, other_c))

            @pl.when(xl != k)
            def _():
                u_send[ubuf(p), :] = src[1, rows_of(p), :].astype(BF)
                cp.start()

            ends.append(unless(xl != k, cp.wait_send))
            msg[f"{N}u{p}"] = cp.wait_recv

        for p in range(8):
            tasks[f"{N}u{p}"] = lambda p=p: ustep(p)

        def zstep(d, i):
            first = 0 if d == "p" else 1
            h = first if i % 2 == 0 else 1 - first
            o = 4 - (i + 1) // 2
            place = PLACE[o if d == "p" or o == 4 else -o]
            mine = zbuf(d, i)
            straight = remote(z_send.at[mine], z_recv.at[mine], zside[d])
            msg[f"{N}r{d}{i}"] = straight.wait_recv
            if h == 1:
                @pl.when(xl == k)
                def _():
                    msg[f"{N}u{place}"]()
                    v = src[1, rows_of(place), :] + u_recv[ubuf(place), :].astype(F32)
                    if i >= 2:
                        msg[f"{N}r{d}{i - 2}"]()
                        v = v + z_recv[zbuf(d, i - 2), :].astype(F32)
                    z_send[mine, :] = v.astype(BF)
                    straight.start()

                ends.append(unless(xl == k, straight.wait_send))
                return
            v = src[0, rows_of(place), :]
            if i >= 2:
                msg[f"{N}r{d}{i - 2}"]()
                v = v + z_recv[zbuf(d, i - 2), :].astype(F32)
            z_send[mine, :] = v.astype(BF)
            if i < 5:
                straight.start()
                ends.append(straight.wait_send)
                return
            there = rows_of(n * 2 + "pm".index(d))
            aslant = remote(z_send.at[mine], s_recv.at[there], slant[d])
            pl.when(xl == k)(straight.start)
            pl.when(xl != k)(aslant.start)
            ends.append(unless(xl == k, straight.wait_send))
            ends.append(unless(xl != k, aslant.wait_send))
            msg[f"{N}s{d}"] = aslant.wait_recv

        for d in "pm":
            for i in range(7):
                tasks[f"{N}r{d}{i}"] = lambda d=d, i=i: zstep(d, i)

        def wstep():
            mine = rows_of(n)
            cp = remote(w_send.at[mine], w_recv.at[mine], (r, other_c))

            @pl.when(xl != k)
            def _():
                w_send[mine, :] = src[0, rows_of(0), :].astype(BF)
                cp.start()

            ends.append(unless(xl != k, cp.wait_send))
            msg[f"{N}w"] = cp.wait_recv

        def tstep(h):
            mine = rows_of(n * 2 + h)
            out = (mixed_out, igrad_out)[n]
            cp = remote(small.at[mine], out, mate)
            stay = pltpu.make_async_copy(small.at[mine], out, lsem.at[count[1]])
            count[1] += 1

            @pl.when(xl == k)
            def _():
                v = src[h, rows_of(0), :]
                if h == 0:
                    msg[f"{N}w"]()
                    v = v + w_recv[rows_of(n), :].astype(F32)
                else:
                    msg[f"{N}u0"]()
                    v = v + u_recv[ubuf(0), :].astype(F32)
                for d in "pm":
                    i = 6 if (h == 0) == (d == "p") else 5
                    msg[f"{N}r{d}{i}"]()
                    v = v + z_recv[zbuf(d, i), :].astype(F32)
                    if h == 0:
                        msg[f"{N}s{d}"]()
                        v = v + s_recv[rows_of(n * 2 + "pm".index(d)), :].astype(F32)
                small[mine, :] = v.astype(BF)
                pl.when(k != h)(cp.start)
                pl.when(k == h)(stay.start)

            give = jnp.logical_and(xl == k, k != h)
            ends.append(unless(give, cp.wait_send))
            ends.append(unless(jnp.logical_and(xl == k, k == h), stay.wait))
            msg[f"{N}t{h}"] = unless(jnp.logical_and(xl != k, k == h), cp.wait_recv)

        def ostep():
            msg[f"{N}t0"]()
            msg[f"{N}t1"]()

        tasks[f"{N}w"] = wstep
        tasks[f"{N}t0"], tasks[f"{N}t1"], tasks[f"{N}o"] = lambda: tstep(0), lambda: tstep(1), ostep

    def forward(v, rows):
        hid[rows, :] = v
        return gelu(v)

    def backward(v, rows):
        return v * gelu_slope(hid[rows, :])

    way(0, "P", tok_source, tok, up, "M", act, down, forward)
    way(1, "Q", grad_source, grad, down_t, "I", hgrad, up_t, backward)

    low, high = pl.ds(0, ROWS), pl.ds(ROWS, ROWS)

    def swap(name, source, buf, out):
        got(*(source(o, h) for o in PLACE for h in (0, 1)))
        send(name, buf.at[1 - k], out, mate)

    tasks["Tm"] = lambda: swap("Tm", tok_source, tok, tok_o)
    tasks["Gm"] = lambda: swap("Gm", grad_source, grad, grad_o)

    def twin(name, buf):
        for h in (0, 1):
            send(f"{name}{h}", buf.at[h, low], buf.at[h, high], mate)

    tasks["Am"] = lambda: twin("Am", act)
    tasks["Hm"] = lambda: twin("Hm", hgrad)

    def outer(a, b):
        return lax.dot_general(a, b, (((0,), (0,)), ((), ())), preferred_element_type=F32)

    def dg(i):
        got("Gm", "Am0", "Am1")
        for h, first, many in (((0, 0, 256),), ((0, 256, 384),), ((1, 0, 256),), ((1, 256, 384),))[i]:
            cols, rows = pl.ds(first, many), pl.ds(h * HALF + first, many)
            v = outer(act[h, low, cols], grad[k]) + outer(act[h, high, cols], grad_o[...])
            downg[rows, :] = v.astype(BF)
            ends.append(lcopy(downg.at[rows], downg_out.at[rows]))

    def ug(i):
        got("Tm", "Hm0", "Hm1")
        rows = pl.ds(*((0, 256), (256, 384))[i])
        for h in (0, 1):
            v = outer(tok[k, :, rows], hgrad[h, low, :]) + outer(tok_o[:, rows], hgrad[h, high, :])
            upg[rows, cols_of(h)] = v.astype(BF)
        ends.append(lcopy(upg.at[rows], upg_out.at[rows]))

    for i in range(4):
        tasks[f"DG{i}"] = lambda i=i: dg(i)
    for i in range(2):
        tasks[f"UG{i}"] = lambda i=i: ug(i)

    for name in ORDER[:-1]:
        tasks[name]()
    for end in ends:
        end()
    ends.clear()
    tasks[ORDER[-1]]()
    for end in ends:
        end()


CUTS = 4


def hand_on(a, b, c, d, a_out, b_out, c_out, d_out, a_mid, b_mid, c_mid, d_mid, in_sem, out_sem):
    ins, outs = [], []
    for src, mid, dst, many in ((c, c_mid, c_out, CUTS), (d, d_mid, d_out, CUTS), (a, a_mid, a_out, 1), (b, b_mid, b_out, 1)):
        rows = src.shape[0] // many
        for i in range(many):
            part = pl.ds(i * rows, rows)
            n = len(ins)
            ins.append(pltpu.make_async_copy(src.at[part], mid.at[part], in_sem.at[n]))
            outs.append(pltpu.make_async_copy(mid.at[part], dst.at[part], out_sem.at[n]))
            ins[n].start()
    for first, then in zip(ins, outs):
        first.wait()
        then.start()
    for cp in outs:
        cp.wait()


def local(tokens, up_weight, down_weight, grad_out):
    vm = pltpu.VMEM
    any_ = pl.BlockSpec(memory_space=pl.ANY)
    done = pl.pallas_call(
        kernel,
        name="ffn",
        out_shape=(
            jax.ShapeDtypeStruct((TOK, HALF), BF),
            jax.ShapeDtypeStruct((TOK, HALF), BF),
            jax.ShapeDtypeStruct((HALF, WIDE), BF),
            jax.ShapeDtypeStruct((WIDE, HALF), BF),
        ),
        in_specs=[any_] * 4,
        out_specs=(any_,) * 4,
        scratch_shapes=[
            vm((WIDE, WIDE), BF), vm((WIDE, WIDE), BF),
            vm((WIDE, WIDE), BF), vm((WIDE, WIDE), BF),
            vm((2, ROWS, HALF), BF), vm((2, ROWS, HALF), BF),
            vm((2, 2 * ROWS, HALF), BF), vm((2, 2 * ROWS, HALF), BF),
            vm((ROWS, HALF), BF), vm((ROWS, HALF), BF),
            vm((2, 2, ROWS, HALF), F32),
            vm((4 * TOK, HALF), F32),
            vm((4 * TOK, HALF), BF), vm((4 * TOK, HALF), BF),
            vm((8 * TOK, HALF), BF), vm((8 * TOK, HALF), BF),
            vm((12 * 128, HALF), BF), vm((12 * 128, HALF), BF),
            vm((28 * TOK, HALF), BF), vm((28 * TOK, HALF), BF),
            vm((16 * TOK, HALF), BF), vm((16 * TOK, HALF), BF),
            vm((4 * TOK, HALF), BF),
            vm((2 * TOK, HALF), BF), vm((2 * TOK, HALF), BF),
            vm((HALF, WIDE), BF), vm((WIDE, HALF), BF),
            vm((4 * TOK, HALF), BF),
            pltpu.SemaphoreType.DMA((192,)),
            pltpu.SemaphoreType.DMA((192,)),
            pltpu.SemaphoreType.DMA((16,)),
        ],
        compiler_params=pltpu.CompilerParams(
            collective_id=0, has_side_effects=True, vmem_limit_bytes=60 * 2**20
        ),
        cost_estimate=pl.CostEstimate(flops=12_600_000_000, bytes_accessed=10_000_000, transcendentals=300_000),
    )(tokens, up_weight, down_weight, grad_out)
    return pl.pallas_call(
        hand_on,
        name="hand_on",
        out_shape=[jax.ShapeDtypeStruct(x.shape, x.dtype) for x in done],
        in_specs=[any_] * 4,
        out_specs=[any_] * 4,
        scratch_shapes=[pltpu.VMEM(x.shape, x.dtype) for x in done]
        + [pltpu.SemaphoreType.DMA((2 * CUTS + 2,))] * 2,
        cost_estimate=pl.CostEstimate(flops=0, bytes_accessed=8_000_000, transcendentals=0),
    )(*done)


def solution(mesh):
    placed = (P("col", "row"), P("row", "col"), P("col", "row"), P("col", "row"))
    return jax.shard_map(
        local,
        mesh=mesh,
        in_specs=placed,
        out_specs=(P("col", "row"), P("col", "row"), P("row", "col"), P("col", "row")),
        check_vma=False,
    )
```
